32 devices in a mesh: grp: 2 (over y), row: 8 (over z, x), col: 2 (over core).
Axes of the slice: x: 2, y: 2, z: 4, core: 2. Of those that a mesh axis runs over, the one named last changes fastest.
Arguments:
- embed: float32 [16, 32, 2048], P(('grp', 'row')), parts along dimension 0, may hold values from -5 to 5
- alpha_solve: float32 [16, 2048], P(('grp', 'row')), parts along dimension 0, may hold values from -8 to 8
- probes: float32 [16, 8, 2048], P(('grp', 'row')), parts along dimension 0, may hold values from -6 to 6
- probe_solves: float32 [16, 8, 2048], P(('grp', 'row')), parts along dimension 0, may hold values from -6 to 6
- counts: int32 [16], P(('grp', 'row')), parts along dimension 0, may hold values from 512 to 2048, as said below
- tile_mask: int32 [16, 9], P(('grp', 'row')), parts along dimension 0, may hold values from 0 to 1, as said below
Outputs:
- grad: float32 [16, 32, 2048], P(('grp', 'row')), parts along dimension 0
The draws below stay inside these ranges and needn't reach their ends.
There are 2 independent parts, one for each index of `grp`. The reference program is written for one: setup_inputs(seed, part) draws one part's arguments, and reference() takes and returns one part's arrays. A program takes and returns all parts, laid end to end along the dimension named above; each array names one. Nothing has to cross between parts.
Inputs may be any that keep to these rules, and one draw needn't show every extreme that they name: symmetric: tile_mask[I, 4 + o] = tile_mask[I + o, 4 - o]; the middle column is 1; entries that name a block outside 0 to 7 are 0. `counts`: some block is full.
All inputs are finite; a program needn't handle non-finite values.
Results may differ from the reference program's by a relative error of at most 0.0003.
Values sent between devices are 32-bit elements; how exact they have to be, the bound alone decides.
No kernel may reach another device: no remote copies, remote signals or barrier semaphores. Data moves between devices by JAX's collectives and lax.ppermute only.
A program may use at most 64 MiB of HBM per device.

```python
import jax
import jax.numpy as jnp
from jax import lax

FEAT = 32
PROBES = 8
BAND = 4
BLOCK = 2048
NB = 8


def draw_counts(key, part):
    key = jax.random.fold_in(key, 11)
    first, second = jax.random.split(key)
    drawn = jax.random.randint(first, (NB,), BLOCK // 4, BLOCK + 1)
    chosen = jax.random.randint(second, (), 0, NB)
    return jnp.where(jnp.arange(NB) == chosen, BLOCK, drawn).astype(jnp.int32)


def draw_tile_mask(key, part):
    key = jax.random.fold_in(key, 23)
    first, second = jax.random.split(key)
    level = jax.random.randint(first, (NB,), 0, 5)
    rolls = jax.random.randint(second, (NB, BAND), 0, 4)
    rows_index = jnp.arange(NB)
    reach = jnp.arange(1, BAND + 1)
    upper = (rolls < level[:, None]) & (rows_index[:, None] + reach[None, :] < NB)
    columns = []
    for offset in range(BAND, 0, -1):
        mirrored = jnp.roll(upper[:, offset - 1], offset) & (rows_index >= offset)
        columns.append(mirrored)
    columns.append(jnp.ones((NB,), bool))
    for offset in range(1, BAND + 1):
        columns.append(upper[:, offset - 1])
    return jnp.stack(columns, axis=1).astype(jnp.int32)


def shard_levels(rng, extent, pieces, low, largest):
    def one(position, parts):
        draws = jax.random.uniform(jax.random.fold_in(jax.random.fold_in(rng, 6), position), (parts,), jnp.float32, low / len(pieces), largest / len(pieces))
        return jnp.repeat(jnp.exp(draws), extent[position] // parts).reshape((-1,) + (1,) * (len(extent) - position - 1))

    gain = one(*pieces[0])
    for cut in pieces[1:]:
        gain = gain * one(*cut)
    return gain


def normal_values(stream_key, extent, deviation, most, pieces=(), kind=jnp.bfloat16):
    entries = deviation * jax.random.normal(stream_key, extent, jnp.float32)
    if pieces:
        entries = entries * shard_levels(stream_key, extent, pieces, -0.22, 0.18)
    return jnp.clip(entries, -most, most).astype(kind)


def setup_inputs(seed: int = 0, part: int = 0) -> dict:
    keys = jax.random.split(jax.random.key(seed), 7)
    own_keys = jax.random.split(jax.random.fold_in(keys[6], part), 7)
    return {
        "embed": normal_values(own_keys[0], (NB, FEAT, BLOCK), 0.8, 5.0, ((0, 8),), jnp.float32),
        "alpha_solve": normal_values(own_keys[1], (NB, BLOCK), 1.5, 8.0, ((0, 8),), jnp.float32),
        "probes": normal_values(own_keys[2], (NB, PROBES, BLOCK), 1.0, 6.0, ((0, 8),), jnp.float32),
        "probe_solves": normal_values(own_keys[3], (NB, PROBES, BLOCK), 1.0, 6.0, ((0, 8),), jnp.float32),
        "counts": draw_counts(jax.random.fold_in(jax.random.fold_in(keys[6], part), 71), part),
        "tile_mask": draw_tile_mask(jax.random.fold_in(jax.random.fold_in(keys[6], part), 71), part),
    }


lengthscale = 7.5

def tile_grad(zi, left, vi, zj, right, vj):
    cross = lax.dot_general(zi, zj, (((0,), (0,)), ((), ())), precision=lax.Precision.HIGHEST)
    norm_rows = lax.optimization_barrier(jnp.sum(zi * zi, axis=0))
    norm_cols = lax.optimization_barrier(jnp.sum(zj * zj, axis=0))
    squared = norm_rows[:, None] + norm_cols[None, :] - 2.0 * cross
    radius = jnp.sqrt(jnp.maximum(squared, 0.0)) / lengthscale
    factor = -20.0 / (lengthscale * lengthscale) * jnp.maximum(1.0 - radius, 0.0) ** 3
    coef = lax.dot_general(left, right, (((0,), (0,)), ((), ())), precision=lax.Precision.HIGHEST)
    weights = coef * factor * vi[:, None] * vj[None, :]
    sums = lax.optimization_barrier(jnp.sum(weights, axis=1))
    mixed = lax.dot_general(zj, weights, (((1,), (1,)), ((), ())), precision=lax.Precision.HIGHEST)
    return zi * sums[None, :] - mixed

def reference(embed, alpha_solve, probes, probe_solves, counts, tile_mask):
    nblocks, feats, block = embed.shape
    nprobe = probes.shape[1]
    scale = 1.0 / (2.0 * nprobe)
    lefts = jnp.concatenate([alpha_solve[:, None, :], probe_solves, probes], axis=1)
    rights = jnp.concatenate([alpha_solve[:, None, :], -scale * probes, -scale * probe_solves], axis=1)
    valid = (jnp.arange(block, dtype=jnp.int32)[None, :] < counts[:, None]).astype(jnp.float32)

    def one_block(index):
        zi = embed[index]
        total = jnp.zeros((feats, block), jnp.float32)
        for offset in range(-BAND, BAND + 1):
            other = index + offset
            inside = (other >= 0) & (other < nblocks)
            picked = jnp.clip(other, 0, nblocks - 1).astype(jnp.int32)
            flag = inside & (tile_mask[index, BAND + offset] > 0)

            def compute():
                return tile_grad(zi, lefts[index], valid[index], embed[picked], rights[picked], valid[picked])

            def nothing():
                return jnp.zeros((feats, block), jnp.float32)
            total = total + lax.cond(flag, compute, nothing)
        return total
    return lax.map(one_block, jnp.arange(nblocks, dtype=jnp.int32))
```

```python
import functools

import jax
import jax.numpy as jnp
from jax import lax
from jax.experimental import pallas as pl
from jax.experimental.pallas import tpu as pltpu
from jax.sharding import PartitionSpec as P

lengthscale = 7.5
f32 = jnp.float32
bf16 = jnp.bfloat16

owner_side = {1: 1, 4: 1, 2: -1, 3: -1}
rounds = ((1, 2), (3, 4))

wide = 256
step_i = 512
step_j = 512
depth_q = 256
depth_c = 128
stack = 80
short = 48


def vmem(count):
    return [pl.BlockSpec(memory_space=pltpu.VMEM)] * count


def smem(count):
    return [pl.BlockSpec(memory_space=pltpu.SMEM)] * count


def split3(value):
    high = value.astype(bf16)
    rest = value - high.astype(f32)
    mid = rest.astype(bf16)
    low = (rest - mid.astype(f32)).astype(bf16)
    return high, mid, low


def split2(value):
    high = value.astype(bf16)
    return high, (value - high.astype(f32)).astype(bf16)


def extra_rows(norms, norms_first):
    high, mid, low = (part.astype(f32) for part in split3(norms))
    width = norms.shape[1]
    index = lax.broadcasted_iota(jnp.int32, (16, width), 0)
    base = 0 if norms_first else 3
    one = 3 - base
    out = jnp.where((index >= one) & (index < one + 3), 1.0, 0.0)
    for place, part in enumerate((high, mid, low)):
        out = jnp.where(index == base + place, part, out)
    return out.astype(bf16)


def distance_rows(z, right):
    high, mid, low = split3(z)
    norms = jnp.sum(z * z, axis=0, keepdims=True)
    if right:
        high, mid, low = (part * jnp.asarray(-2.0, bf16) for part in (high, mid, low))
        parts = [high, mid, high, low, high, mid]
    else:
        parts = [high, high, mid, high, low, mid]
    pad = jnp.zeros((depth_q - 6 * z.shape[0] - 16, z.shape[1]), bf16)
    return jnp.concatenate(parts + [extra_rows(norms, not right), pad], axis=0)


def coef_rows(alpha, solves, probes, right):
    nprobe = probes.shape[0]
    width = probes.shape[1]
    pad = jnp.zeros((32 - 2 * nprobe - 8, width), f32)
    index = lax.broadcasted_iota(jnp.int32, (8, width), 0)
    if right:
        gain = -20.0 / lengthscale
        scale = -gain / (2.0 * nprobe)
        top = [scale * probes, scale * solves]
        alpha = gain * alpha
    else:
        top = [solves, probes]
    last = jnp.where(index == 0, alpha, 0.0)
    value = jnp.concatenate(top + [last, pad], axis=0)
    high, low = split2(value)
    parts = [high, low, high] if right else [high, high, low]
    fill = jnp.zeros((depth_c - 96, width), bf16)
    return jnp.concatenate(parts + [fill], axis=0)


def stack_rows(z):
    high, low = split2(z)
    index = lax.broadcasted_iota(jnp.int32, (16, z.shape[1]), 0)
    ones = jnp.where(index == 0, 1.0, 0.0).astype(bf16)
    return jnp.concatenate([high, ones, low], axis=0)


def pack_kernel(count_ref, embed_ref, alpha_ref, probes_ref, solves_ref, out_ref):
    feats, block = embed_ref.shape[1:]
    tiles = block // 128
    count = count_ref[0]
    place = 0
    for ref, scale in ((embed_ref, 1.0 / lengthscale), (solves_ref, None), (probes_ref, None)):
        for group in range(ref.shape[1] // 8):
            for tile in range(tiles):
                value = ref[0, 8 * group : 8 * group + 8, 128 * tile : 128 * tile + 128]
                if scale is None:
                    index = lax.broadcasted_iota(jnp.int32, (8, 128), 1) + 128 * tile
                    value = jnp.where(index < count, value, 0.0)
                else:
                    value = value * scale
                out_ref[place : place + 8, :] = value
                place += 8
    for tile in range(tiles):
        value = alpha_ref[:, 128 * tile : 128 * tile + 128]
        index = lax.broadcasted_iota(jnp.int32, (1, 128), 1) + 128 * tile
        out_ref[place : place + 1, :] = jnp.where(index < count, value, 0.0)
        place += 1
    out_ref[place : place + 8, :] = jnp.full((8, 128), 1.0, f32) * count.astype(f32)


def packed_rows(feats, nprobe, block):
    return (feats + 2 * nprobe) * block // 128 + block // 128 + 8


def chunk_of(ref, chunk, feats, nprobe, block):
    tiles = block // 128
    first = chunk * (wide // 128)

    def rows(start):
        pieces = []
        for tile in range(wide // 128):
            at = pl.multiple_of(8 * (start * tiles + first + tile), 8)
            pieces.append(ref[pl.ds(at, 8), :])
        return jnp.concatenate(pieces, axis=1)

    groups = feats // 8
    z = jnp.concatenate([rows(group) for group in range(groups)], axis=0)
    solves = jnp.concatenate([rows(groups + g) for g in range(nprobe // 8)], axis=0)
    probes = jnp.concatenate([rows(groups + nprobe // 8 + g) for g in range(nprobe // 8)], axis=0)
    base = 8 * (groups + 2 * (nprobe // 8)) * tiles
    alpha = jnp.concatenate(
        [ref[pl.ds(base + first + tile, 1), :] for tile in range(wide // 128)], axis=1
    )
    return z, alpha, solves, probes


def fill_right(ref, chunk, sizes, right_q, right_c, zs, zf):
    feats, nprobe, block = sizes
    z, alpha, solves, probes = chunk_of(ref, chunk, feats, nprobe, block)
    at = pl.ds(pl.multiple_of(chunk * wide, wide), wide)
    right_q[:, at] = distance_rows(z, True)
    right_c[:, at] = coef_rows(alpha, solves, probes, True)
    zs[:, at] = stack_rows(z)
    zf[:, at] = z


def fill_left(ref, chunk, sizes, left_q, left_c):
    feats, nprobe, block = sizes
    z, alpha, solves, probes = chunk_of(ref, chunk, feats, nprobe, block)
    at = pl.ds(pl.multiple_of(chunk * wide, wide), wide)
    left_q[at, :] = distance_rows(z, False).T
    left_c[at, :] = coef_rows(alpha, solves, probes, False).T


def weights(left_q, left_c, right_q, right_c, at_j, at_i):
    squared = jnp.dot(left_q[at_j, :], right_q[:, at_i], preferred_element_type=f32)
    coef = jnp.dot(left_c[at_j, :], right_c[:, at_i], preferred_element_type=f32)
    squared = jnp.maximum(squared, 1e-30)
    radius = squared * lax.rsqrt(squared)
    rest = jnp.maximum(1.0 - radius, 0.0)
    return rest * rest * rest * coef


over_lanes = (((1,), (1,)), ((), ()))


def add_right(total, zs, at_j, at_i, high, low):
    total[:, at_i] += jnp.dot(zs[:, at_j], high, preferred_element_type=f32)
    total[:short, at_i] += jnp.dot(zs[:short, at_j], low, preferred_element_type=f32)


def add_left(total, zs, at_j, at_i, high, low):
    total[:, at_j] += lax.dot_general(zs[:, at_i], high, over_lanes, preferred_element_type=f32)
    total[:short, at_j] += lax.dot_general(
        zs[:short, at_i], low, over_lanes, preferred_element_type=f32
    )


def finish(z, total, feats):
    return z * total[feats : feats + 1, :] - (total[:feats, :] + total[short : short + feats, :])


def at_chunk(index, size):
    return pl.ds(pl.multiple_of(index * size, size), size)


def own_kernel(sizes, control, packed, left_q, left_c, zs, zf, grad, right_q, right_c, total):
    feats, nprobe, block = sizes
    for chunk in range(block // wide):
        fill_left(packed, chunk, sizes, left_q, left_c)
        fill_right(packed, chunk, sizes, right_q, right_c, zs, zf)
    total[...] = jnp.zeros_like(total)
    count, start, stride = control[0], control[1], control[2]
    steps = (count + step_i - 1) // step_i

    def one_row(j, carry):
        def one(i, inner):
            @pl.when((i + j) % stride == start)
            def _():
                at_j, at_i = at_chunk(j, step_i), at_chunk(i, step_i)
                high, low = split2(weights(left_q, left_c, right_q, right_c, at_j, at_i))
                add_right(total, zs, at_j, at_i, high, low)

                @pl.when(i > j)
                def _():
                    add_left(total, zs, at_j, at_i, high, low)

            return inner

        return lax.fori_loop(j, steps, one, carry)

    lax.fori_loop(0, steps, one_row, 0)
    grad[...] = finish(zf[...], total[...], feats)


def pair_kernel(
    sizes, control, packed, left_q, left_c, zs, zf, grad_in, grad, back, right_q, right_c, zsp, zfp, total, totalp
):
    feats, nprobe, block = sizes
    base = packed.shape[0] - 8
    other = jnp.max(packed[base : base + 8, :]).astype(jnp.int32)
    live = control[1]
    steps_i = live * ((other + step_i - 1) // step_i)
    steps_j = (control[0] + step_j - 1) // step_j

    @pl.when(steps_i == 0)
    def _():
        grad[...] = grad_in[...]
        back[...] = jnp.zeros_like(back)

    @pl.when(steps_i > 0)
    def _():
        total[...] = jnp.zeros_like(total)
        totalp[...] = jnp.zeros_like(totalp)
        for chunk in range(block // wide):
            fill_right(packed, chunk, sizes, right_q, right_c, zsp, zfp)

        def one_row(i, carry):
            def one(j, inner):
                at_j, at_i = at_chunk(j, step_j), at_chunk(i, step_i)
                high, low = split2(weights(left_q, left_c, right_q, right_c, at_j, at_i))
                add_right(totalp, zs, at_j, at_i, high, low)
                add_left(total, zsp, at_j, at_i, high, low)
                return inner

            return lax.fori_loop(0, steps_j, one, carry)

        lax.fori_loop(0, steps_i, one_row, 0)
        grad[...] = grad_in[...] + finish(zf[...], total[...], feats)
        back[...] = finish(zfp[...], totalp[...], feats)


def shape(*dims, dtype=f32):
    return jax.ShapeDtypeStruct(dims, dtype)


params = pltpu.CompilerParams(vmem_limit_bytes=48 << 20)


def pair_list(rows, cores, offsets, back):
    pairs = []
    for row in range(rows):
        for core in range(cores):
            offset = offsets[core]
            source = row + owner_side[offset] * offset
            if 0 <= source < rows:
                there, here = source * cores + core, row * cores + core
                pairs.append((here, there) if back else (there, here))
    return pairs


def local(embed, alpha_solve, probes, probe_solves, counts, tile_mask):
    feats, block = embed.shape[1:]
    nprobe = probes.shape[1]
    band = (tile_mask.shape[1] - 1) // 2
    sizes = (feats, nprobe, block)
    rows, cores = lax.axis_size("row"), lax.axis_size("col")
    core = lax.axis_index("col")

    packed = pl.pallas_call(
        pack_kernel,
        out_shape=shape(packed_rows(feats, nprobe, block), 128),
        in_specs=smem(1) + vmem(4),
        out_specs=pl.BlockSpec(memory_space=pltpu.VMEM),
        compiler_params=params,
        name="pack",
    )(counts, embed, alpha_solve, probes, probe_solves)

    arrived = [
        lax.ppermute(packed, ("row", "col"), pair_list(rows, cores, offsets, False))
        for offsets in rounds
    ]

    def live(offset):
        return (tile_mask[0, band + owner_side[offset] * offset] > 0).astype(jnp.int32)

    loads = [sum(live(offsets[which]) for offsets in rounds) for which in range(2)]
    stride = jnp.where(loads[0] == loads[1], 2, 1)
    lighter = jnp.where(loads[0] < loads[1], 0, 1)
    start = jnp.where(stride == 2, core, jnp.where(lighter == core, 0, 1))
    control = jnp.stack([counts[0], start, stride]).astype(jnp.int32)

    operands = (
        shape(block, depth_q, dtype=bf16),
        shape(block, depth_c, dtype=bf16),
        shape(stack, block, dtype=bf16),
        shape(feats, block),
    )
    scratch = [
        pltpu.VMEM((depth_q, block), bf16),
        pltpu.VMEM((depth_c, block), bf16),
    ]
    *own, grad = pl.pallas_call(
        functools.partial(own_kernel, sizes),
        out_shape=operands + (shape(feats, block),),
        in_specs=smem(1) + vmem(1),
        out_specs=tuple(vmem(5)),
        scratch_shapes=scratch + [pltpu.VMEM((stack, block), f32)],
        compiler_params=params,
        cost_estimate=pl.CostEstimate(flops=8 << 30, bytes_accessed=4 << 20, transcendentals=2 << 20),
        name="own_tile",
    )(control, packed)

    returned = []
    for offsets, payload in zip(rounds, arrived):
        flag = jnp.where(core == 0, live(offsets[0]), live(offsets[1]))
        grad, back = pl.pallas_call(
            functools.partial(pair_kernel, sizes),
            out_shape=(shape(feats, block), shape(feats, block)),
            in_specs=smem(1) + vmem(6),
            out_specs=tuple(vmem(2)),
            scratch_shapes=scratch
            + [
                pltpu.VMEM((stack, block), bf16),
                pltpu.VMEM((feats, block), f32),
                pltpu.VMEM((stack, block), f32),
                pltpu.VMEM((stack, block), f32),
            ],
            compiler_params=params,
            cost_estimate=pl.CostEstimate(
                flops=8 << 30, bytes_accessed=4 << 20, transcendentals=2 << 20
            ),
            name="pair_tile",
        )(jnp.stack([counts[0], flag]), payload, *own, grad)
        returned.append(lax.ppermute(back, ("row", "col"), pair_list(rows, cores, offsets, True)))
    total = grad + returned[0] + returned[1]
    total = total + lax.ppermute(total, "col", [(0, 1), (1, 0)])
    return total[None]


def solution(mesh):
    in_specs = (
        P(("grp", "row"), None, None),
        P(("grp", "row"), None),
        P(("grp", "row"), None, None),
        P(("grp", "row"), None, None),
        P(("grp", "row")),
        P(("grp", "row"), None),
    )
    out_specs = P(("grp", "row"), None, None)
    return jax.shard_map(local, mesh=mesh, in_specs=in_specs, out_specs=out_specs, check_vma=False)
```

```python
import functools

import jax
import jax.numpy as jnp
from jax import lax
from jax.experimental import pallas as pl
from jax.experimental.pallas import tpu as pltpu
from jax.sharding import PartitionSpec as P

lengthscale = 7.5
f32 = jnp.float32
bf16 = jnp.bfloat16

owner_side = {1: 1, 4: 1, 2: -1, 3: -1}
rounds = ((1, 2), (3, 4))

wide = 256
step_i = 256
step_j = 512
depth_q = 256
depth_c = 128
stack = 80
short = 48


def vmem(count):
    return [pl.BlockSpec(memory_space=pltpu.VMEM)] * count


def smem(count):
    return [pl.BlockSpec(memory_space=pltpu.SMEM)] * count


def split3(value):
    high = value.astype(bf16)
    rest = value - high.astype(f32)
    mid = rest.astype(bf16)
    low = (rest - mid.astype(f32)).astype(bf16)
    return high, mid, low


def split2(value):
    high = value.astype(bf16)
    return high, (value - high.astype(f32)).astype(bf16)


def extra_rows(norms, norms_first):
    high, mid, low = (part.astype(f32) for part in split3(norms))
    width = norms.shape[1]
    index = lax.broadcasted_iota(jnp.int32, (16, width), 0)
    base = 0 if norms_first else 3
    one = 3 - base
    out = jnp.where((index >= one) & (index < one + 3), 1.0, 0.0)
    for place, part in enumerate((high, mid, low)):
        out = jnp.where(index == base + place, part, out)
    return out.astype(bf16)


def distance_rows(z, right):
    high, mid, low = split3(z)
    norms = jnp.sum(z * z, axis=0, keepdims=True)
    if right:
        high, mid, low = (part * jnp.asarray(-2.0, bf16) for part in (high, mid, low))
        parts = [high, mid, high, low, high, mid]
    else:
        parts = [high, high, mid, high, low, mid]
    pad = jnp.zeros((depth_q - 6 * z.shape[0] - 16, z.shape[1]), bf16)
    return jnp.concatenate(parts + [extra_rows(norms, not right), pad], axis=0)


def coef_rows(alpha, solves, probes, right):
    nprobe = probes.shape[0]
    width = probes.shape[1]
    pad = jnp.zeros((32 - 2 * nprobe - 8, width), f32)
    index = lax.broadcasted_iota(jnp.int32, (8, width), 0)
    if right:
        gain = -20.0 / lengthscale
        scale = -gain / (2.0 * nprobe)
        top = [scale * probes, scale * solves]
        alpha = gain * alpha
    else:
        top = [solves, probes]
    last = jnp.where(index == 0, alpha, 0.0)
    value = jnp.concatenate(top + [last, pad], axis=0)
    high, low = split2(value)
    parts = [high, low, high] if right else [high, high, low]
    fill = jnp.zeros((depth_c - 96, width), bf16)
    return jnp.concatenate(parts + [fill], axis=0)


def stack_rows(z):
    high, low = split2(z)
    index = lax.broadcasted_iota(jnp.int32, (16, z.shape[1]), 0)
    ones = jnp.where(index == 0, 1.0, 0.0).astype(bf16)
    return jnp.concatenate([high, ones, low], axis=0)


def pack_kernel(count_hbm, embed_hbm, alpha_hbm, probes_hbm, solves_hbm, out_ref, *scratch):
    count_ref, embed_ref, alpha_ref, probes_ref, solves_ref, done = scratch
    sources = (count_hbm, embed_hbm, alpha_hbm, probes_hbm, solves_hbm)
    copies = [
        pltpu.make_async_copy(source, target, done.at[place])
        for place, (source, target) in enumerate(zip(sources, scratch[:5]))
    ]
    for copy in copies:
        copy.start()
    for copy in copies:
        copy.wait()
    tiles = embed_ref.shape[2] // 128
    count = count_ref[0]
    place = 0
    for ref, scale in ((embed_ref, 1.0 / lengthscale), (solves_ref, None), (probes_ref, None)):
        for group in range(ref.shape[1] // 8):
            for tile in range(tiles):
                value = ref[0, 8 * group : 8 * group + 8, 128 * tile : 128 * tile + 128]
                if scale is None:
                    index = lax.broadcasted_iota(jnp.int32, (8, 128), 1) + 128 * tile
                    value = jnp.where(index < count, value, 0.0)
                else:
                    value = value * scale
                out_ref[place : place + 8, :] = value
                place += 8
    for tile in range(tiles):
        value = alpha_ref[:, 128 * tile : 128 * tile + 128]
        index = lax.broadcasted_iota(jnp.int32, (1, 128), 1) + 128 * tile
        out_ref[place : place + 1, :] = jnp.where(index < count, value, 0.0)
        place += 1
    out_ref[place : place + 8, :] = jnp.full((8, 128), 1.0, f32) * count.astype(f32)


def call_pack(counts, embed, alpha_solve, probes, probe_solves):
    feats, block = embed.shape[1:]
    values = (embed, alpha_solve, probes, probe_solves)
    return pl.pallas_call(
        pack_kernel,
        out_shape=shape(packed_rows(feats, probes.shape[1], block), 128),
        in_specs=[pl.BlockSpec(memory_space=pltpu.HBM)] * 5,
        out_specs=pl.BlockSpec(memory_space=pltpu.VMEM),
        scratch_shapes=[pltpu.SMEM(counts.shape, jnp.int32)]
        + [pltpu.VMEM(value.shape, f32) for value in values]
        + [pltpu.SemaphoreType.DMA((5,))],
        compiler_params=params,
        name="pack",
    )(counts, *values)


def packed_rows(feats, nprobe, block):
    return (feats + 2 * nprobe) * block // 128 + block // 128 + 8


def chunk_of(ref, chunk, feats, nprobe, block):
    tiles = block // 128
    first = chunk * (wide // 128)

    def rows(start):
        pieces = []
        for tile in range(wide // 128):
            at = pl.multiple_of(8 * (start * tiles + first + tile), 8)
            pieces.append(ref[pl.ds(at, 8), :])
        return jnp.concatenate(pieces, axis=1)

    groups = feats // 8
    z = jnp.concatenate([rows(group) for group in range(groups)], axis=0)
    solves = jnp.concatenate([rows(groups + g) for g in range(nprobe // 8)], axis=0)
    probes = jnp.concatenate([rows(groups + nprobe // 8 + g) for g in range(nprobe // 8)], axis=0)
    base = 8 * (groups + 2 * (nprobe // 8)) * tiles
    alpha = jnp.concatenate(
        [ref[pl.ds(base + first + tile, 1), :] for tile in range(wide // 128)], axis=1
    )
    return z, alpha, solves, probes


def fill_right(ref, chunk, sizes, right_q, right_c, zs):
    feats, nprobe, block = sizes
    z, alpha, solves, probes = chunk_of(ref, chunk, feats, nprobe, block)
    at = pl.ds(pl.multiple_of(chunk * wide, wide), wide)
    right_q[:, at] = distance_rows(z, True)
    right_c[:, at] = coef_rows(alpha, solves, probes, True)
    zs[:, at] = stack_rows(z)


def fill_left(ref, chunk, sizes, left_q, left_c):
    feats, nprobe, block = sizes
    z, alpha, solves, probes = chunk_of(ref, chunk, feats, nprobe, block)
    at = pl.ds(pl.multiple_of(chunk * wide, wide), wide)
    left_q[at, :] = distance_rows(z, False).T
    left_c[at, :] = coef_rows(alpha, solves, probes, False).T


def products(left_q, left_c, right_q, right_c, at_j, at_i):
    squared = jnp.dot(left_q[at_j, :], right_q[:, at_i], preferred_element_type=f32)
    coef = jnp.dot(left_c[at_j, :], right_c[:, at_i], preferred_element_type=f32)
    return squared, coef


def weigh(squared, coef):
    squared = jnp.maximum(squared, 1e-30)
    radius = squared * lax.rsqrt(squared)
    rest = jnp.maximum(1.0 - radius, 0.0)
    return rest * rest * rest * coef


def weights(left_q, left_c, right_q, right_c, at_j, at_i):
    return weigh(*products(left_q, left_c, right_q, right_c, at_j, at_i))


over_lanes = (((1,), (1,)), ((), ()))


def add_right(total, zs, at_j, at_i, high, low):
    total[:, at_i] += jnp.dot(zs[:, at_j], high, preferred_element_type=f32)
    total[:short, at_i] += jnp.dot(zs[:short, at_j], low, preferred_element_type=f32)


def add_left(total, zst, at_j, at_i, high, low):
    z = zst[at_i, :]
    both = jnp.concatenate([high, low], axis=1)
    total[at_j, :] += jnp.dot(both, jnp.concatenate([z, z], axis=0), preferred_element_type=f32)


def fill_stack_t(zst, zs, chunk):
    at = pl.ds(pl.multiple_of(chunk * wide, wide), wide)
    pad = jnp.zeros((128 - stack, wide), bf16)
    zst[at, :] = jnp.concatenate([zs[:, at], pad], axis=0).T


def finish_left(z, total, feats):
    return finish(z, total[...].T, feats)


def finish(z, total, feats):
    return z * total[feats : feats + 1, :] - (total[:feats, :] + total[short : short + feats, :])


def at_chunk(index, size):
    return pl.ds(pl.multiple_of(index * size, size), size)


def pipeline(first, steps, begin, use, even, odd):
    def store(slot, parts):
        high, low = split2(weigh(*parts))
        slot[0][...] = high
        slot[1][...] = low

    def two(pair, carry):
        step = first + 2 * pair
        parts = begin(step + 1)
        use(step, even)
        store(odd, parts)
        parts = begin(step + 2)
        use(step + 1, odd)
        store(even, parts)
        return carry

    def four(quad, carry):
        two(2 * quad, carry)
        return two(2 * quad + 1, carry)

    pairs = (steps - 1) // 2
    last = first + steps - 1
    store(even, begin(first))
    lax.fori_loop(0, pairs // 2, four, 0)
    lax.fori_loop(pairs // 2 * 2, pairs, two, 0)

    @pl.when(steps == 2 * pairs + 2)
    def _():
        parts = begin(last)
        use(last - 1, even)
        store(odd, parts)
        use(last, odd)

    @pl.when(steps == 2 * pairs + 1)
    def _():
        use(last, even)


def steps_of(count, size):
    return (count + size - 1) // size


def live_flag(mask, offset):
    band = (mask.shape[1] - 1) // 2
    return jnp.where(mask[0, band + owner_side[offset] * offset] > 0, 1, 0)


def own_kernel(sizes, counts, mask, packed, left_q, left_c, zs, zf, grad, right_q, right_c, total, *slots):
    feats, nprobe, block = sizes
    count = counts[0]
    steps_i, steps_j = steps_of(count, step_i), steps_of(count, step_j)
    for chunk in range(block // wide):
        zf[:, chunk * wide : chunk * wide + wide] = chunk_of(packed, chunk, feats, nprobe, block)[0]

    def prepare(chunk, carry):
        fill_left(packed, chunk, sizes, left_q, left_c)
        fill_right(packed, chunk, sizes, right_q, right_c, zs)
        return carry

    lax.fori_loop(0, steps_j * (step_j // wide), prepare, 0)
    total[...] = jnp.zeros_like(total)

    core = lax.axis_index("col")
    loads = [sum(live_flag(mask, offsets[which]) for offsets in rounds) for which in range(2)]
    steps = steps_i * steps_j
    half = steps // 2
    mine = jnp.where(core == 0, loads[0], loads[1])
    theirs = jnp.where(core == 0, loads[1], loads[0])
    first = jnp.where((mine == theirs) & (core == 1), half, 0)
    end = jnp.where((mine == theirs) & (core == 0), half, jnp.where(mine > theirs, 0, steps))

    def places(step):
        i = step // steps_j
        return at_chunk(step - i * steps_j, step_j), at_chunk(i, step_i)

    def begin(step):
        return products(left_q, left_c, right_q, right_c, *places(step))

    def use(step, slot):
        at_j, at_i = places(step)
        add_right(total, zs, at_j, at_i, slot[0][...], slot[1][...])

    @pl.when(end > first)
    def _():
        pipeline(first, end - first, begin, use, slots[:2], slots[2:])

    grad[...] = finish(zf[...], total[...], feats)


def pair_kernel(
    sizes, offsets, counts, mask, packed, left_q, left_c, zs, zf, grad_in, grad, back, right_q, right_c, zsp, zfp, total, totalp, zst, *slots
):
    feats, nprobe, block = sizes
    base = packed.shape[0] - 8
    other = jnp.max(packed[base : base + 8, :]).astype(jnp.int32)
    live = jnp.where(lax.axis_index("col") == 0, live_flag(mask, offsets[0]), live_flag(mask, offsets[1]))
    steps_i = live * steps_of(other, step_i)
    steps_j = steps_of(counts[0], step_j)

    @pl.when(steps_i == 0)
    def _():
        grad[...] = grad_in[...]
        back[...] = jnp.zeros_like(back)

    @pl.when(steps_i > 0)
    def _():
        total[...] = jnp.zeros_like(total)
        totalp[...] = jnp.zeros_like(totalp)
        for chunk in range(block // wide):
            zfp[:, chunk * wide : chunk * wide + wide] = chunk_of(packed, chunk, feats, nprobe, block)[0]

        def prepare(chunk, carry):
            fill_right(packed, chunk, sizes, right_q, right_c, zsp)
            fill_stack_t(zst, zsp, chunk)
            return carry

        lax.fori_loop(0, steps_i * (step_i // wide), prepare, 0)

        def places(step):
            i = step // steps_j
            return at_chunk(step - i * steps_j, step_j), at_chunk(i, step_i)

        def begin(step):
            return products(left_q, left_c, right_q, right_c, *places(step))

        def use(step, slot):
            at_j, at_i = places(step)
            high, low = slot[0][...], slot[1][...]
            add_right(totalp, zs, at_j, at_i, high, low)
            add_left(total, zst, at_j, at_i, high, low)

        pipeline(0, steps_i * steps_j, begin, use, slots[:2], slots[2:])
        grad[...] = grad_in[...] + finish_left(zf[...], total, feats)
        back[...] = finish(zfp[...], totalp[...], feats)


def shape(*dims, dtype=f32):
    return jax.ShapeDtypeStruct(dims, dtype)


params = pltpu.CompilerParams(vmem_limit_bytes=32 << 20)
estimate = pl.CostEstimate(flops=8 << 30, bytes_accessed=4 << 20, transcendentals=2 << 20)


slot_scratch = [pltpu.VMEM((step_j, step_i), bf16)] * 4


def call_own(counts, mask, packed, sizes):
    feats, nprobe, block = sizes
    operands = (
        shape(block, depth_q, dtype=bf16),
        shape(block, depth_c, dtype=bf16),
        shape(stack, block, dtype=bf16),
        shape(feats, block),
    )
    *own, grad = pl.pallas_call(
        functools.partial(own_kernel, sizes),
        out_shape=operands + (shape(feats, block),),
        in_specs=smem(2) + vmem(1),
        out_specs=tuple(vmem(5)),
        scratch_shapes=[
            pltpu.VMEM((depth_q, block), bf16),
            pltpu.VMEM((depth_c, block), bf16),
            pltpu.VMEM((stack, block), f32),
        ]
        + slot_scratch,
        compiler_params=params,
        cost_estimate=estimate,
        name="own_tile",
    )(counts, mask, packed)
    return own, grad


def call_pair(counts, mask, payload, own, grad, sizes, offsets):
    feats, nprobe, block = sizes
    return pl.pallas_call(
        functools.partial(pair_kernel, sizes, offsets),
        out_shape=(shape(feats, block), shape(feats, block)),
        in_specs=smem(2) + vmem(6),
        out_specs=tuple(vmem(2)),
        scratch_shapes=[
            pltpu.VMEM((depth_q, block), bf16),
            pltpu.VMEM((depth_c, block), bf16),
            pltpu.VMEM((stack, block), bf16),
            pltpu.VMEM((feats, block), f32),
            pltpu.VMEM((block, 128), f32),
            pltpu.VMEM((stack, block), f32),
            pltpu.VMEM((block, 128), bf16),
        ]
        + slot_scratch,
        compiler_params=params,
        cost_estimate=estimate,
        name="pair_tile",
    )(counts, mask, payload, *own, grad)


def pair_list(rows, cores, offsets, back):
    pairs = []
    for row in range(rows):
        for core in range(cores):
            offset = offsets[core]
            source = row + owner_side[offset] * offset
            if 0 <= source < rows:
                there, here = source * cores + core, row * cores + core
                pairs.append((here, there) if back else (there, here))
    return pairs


def local(embed, alpha_solve, probes, probe_solves, counts, tile_mask):
    feats, block = embed.shape[1:]
    sizes = (feats, probes.shape[1], block)
    rows, cores = lax.axis_size("row"), lax.axis_size("col")
    packed = call_pack(counts, embed, alpha_solve, probes, probe_solves)
    arrived = [
        lax.ppermute(packed, ("row", "col"), pair_list(rows, cores, offsets, False))
        for offsets in rounds
    ]
    own, grad = call_own(counts, tile_mask, packed, sizes)
    returned = []
    for offsets, payload in zip(rounds, arrived):
        grad, back = call_pair(counts, tile_mask, payload, own, grad, sizes, offsets)
        returned.append(lax.ppermute(back, ("row", "col"), pair_list(rows, cores, offsets, True)))
    total = grad + returned[0] + returned[1]
    total = total + lax.ppermute(total, "col", [(0, 1), (1, 0)])
    return total[None]


def solution(mesh):
    in_specs = (
        P(("grp", "row"), None, None),
        P(("grp", "row"), None),
        P(("grp", "row"), None, None),
        P(("grp", "row"), None, None),
        P(("grp", "row")),
        P(("grp", "row"), None),
    )
    out_specs = P(("grp", "row"), None, None)
    return jax.shard_map(local, mesh=mesh, in_specs=in_specs, out_specs=out_specs, check_vma=False)
```

```python
import functools

import jax
import jax.numpy as jnp
from jax import lax
from jax.experimental import pallas as pl
from jax.experimental.pallas import tpu as pltpu
from jax.sharding import PartitionSpec as P

lengthscale = 7.5
f32 = jnp.float32
bf16 = jnp.bfloat16

owner_side = {1: 1, 4: 1, 2: -1, 3: -1}
rounds = ((1, 2), (3, 4))

wide = 256
step_i = 256
step_j = 512
early = 6
depth_q = 256
depth_c = 128
stack = 80
short = 48


def vmem(count):
    return [pl.BlockSpec(memory_space=pltpu.VMEM)] * count


def smem(count):
    return [pl.BlockSpec(memory_space=pltpu.SMEM)] * count


def split3(value):
    high = value.astype(bf16)
    rest = value - high.astype(f32)
    mid = rest.astype(bf16)
    low = (rest - mid.astype(f32)).astype(bf16)
    return high, mid, low


def split2(value):
    high = value.astype(bf16)
    return high, (value - high.astype(f32)).astype(bf16)


def extra_rows(norms, norms_first):
    high, mid, low = (part.astype(f32) for part in split3(norms))
    width = norms.shape[1]
    index = lax.broadcasted_iota(jnp.int32, (16, width), 0)
    base = 0 if norms_first else 3
    one = 3 - base
    out = jnp.where((index >= one) & (index < one + 3), 1.0, 0.0)
    for place, part in enumerate((high, mid, low)):
        out = jnp.where(index == base + place, part, out)
    return out.astype(bf16)


def distance_rows(z, right):
    high, mid, low = split3(z)
    norms = jnp.sum(z * z, axis=0, keepdims=True)
    if right:
        high, mid, low = (part * jnp.asarray(-2.0, bf16) for part in (high, mid, low))
        parts = [high, mid, high, low, high, mid]
    else:
        parts = [high, high, mid, high, low, mid]
    pad = jnp.zeros((depth_q - 6 * z.shape[0] - 16, z.shape[1]), bf16)
    return jnp.concatenate(parts + [extra_rows(norms, not right), pad], axis=0)


def coef_rows(alpha, solves, probes, right):
    nprobe = probes.shape[0]
    width = probes.shape[1]
    pad = jnp.zeros((32 - 2 * nprobe - 8, width), f32)
    index = lax.broadcasted_iota(jnp.int32, (8, width), 0)
    if right:
        gain = -20.0 / lengthscale
        scale = -gain / (2.0 * nprobe)
        top = [scale * probes, scale * solves]
        alpha = gain * alpha
    else:
        top = [solves, probes]
    last = jnp.where(index == 0, alpha, 0.0)
    value = jnp.concatenate(top + [last, pad], axis=0)
    high, low = split2(value)
    parts = [high, low, high] if right else [high, high, low]
    fill = jnp.zeros((depth_c - 96, width), bf16)
    return jnp.concatenate(parts + [fill], axis=0)


def stack_rows(z):
    high, low = split2(z)
    index = lax.broadcasted_iota(jnp.int32, (16, z.shape[1]), 0)
    ones = jnp.where(index == 0, 1.0, 0.0).astype(bf16)
    return jnp.concatenate([high, ones, low], axis=0)


def pack_kernel(count_hbm, embed_hbm, alpha_hbm, probes_hbm, solves_hbm, out_ref, *scratch):
    count_ref, embed_ref, alpha_ref, probes_ref, solves_ref, done = scratch
    sources = (count_hbm, embed_hbm, alpha_hbm, probes_hbm, solves_hbm)
    copies = [
        pltpu.make_async_copy(source, target, done.at[place])
        for place, (source, target) in enumerate(zip(sources, scratch[:5]))
    ]
    for copy in copies:
        copy.start()
    for copy in copies:
        copy.wait()
    tiles = embed_ref.shape[2] // 128
    count = count_ref[0]
    place = 0
    for ref, scale in ((embed_ref, 1.0 / lengthscale), (solves_ref, None), (probes_ref, None)):
        for group in range(ref.shape[1] // 8):
            for tile in range(tiles):
                value = ref[0, 8 * group : 8 * group + 8, 128 * tile : 128 * tile + 128]
                if scale is None:
                    index = lax.broadcasted_iota(jnp.int32, (8, 128), 1) + 128 * tile
                    value = jnp.where(index < count, value, 0.0)
                else:
                    value = value * scale
                out_ref[place : place + 8, :] = value
                place += 8
    for tile in range(tiles):
        value = alpha_ref[:, 128 * tile : 128 * tile + 128]
        index = lax.broadcasted_iota(jnp.int32, (1, 128), 1) + 128 * tile
        out_ref[place : place + 1, :] = jnp.where(index < count, value, 0.0)
        place += 1
    out_ref[place : place + 8, :] = jnp.full((8, 128), 1.0, f32) * count.astype(f32)


def call_pack(counts, embed, alpha_solve, probes, probe_solves):
    feats, block = embed.shape[1:]
    values = (embed, alpha_solve, probes, probe_solves)
    return pl.pallas_call(
        pack_kernel,
        out_shape=shape(packed_rows(feats, probes.shape[1], block), 128),
        in_specs=[pl.BlockSpec(memory_space=pltpu.HBM)] * 5,
        out_specs=pl.BlockSpec(memory_space=pltpu.VMEM),
        scratch_shapes=[pltpu.SMEM(counts.shape, jnp.int32)]
        + [pltpu.VMEM(value.shape, f32) for value in values]
        + [pltpu.SemaphoreType.DMA((5,))],
        compiler_params=pltpu.CompilerParams(vmem_limit_bytes=62 << 20),
        name="pack",
    )(counts, *values)


def packed_rows(feats, nprobe, block):
    return (feats + 2 * nprobe) * block // 128 + block // 128 + 8


def chunk_of(ref, chunk, feats, nprobe, block):
    tiles = block // 128
    first = chunk * (wide // 128)

    def rows(start):
        pieces = []
        for tile in range(wide // 128):
            at = pl.multiple_of(8 * (start * tiles + first + tile), 8)
            pieces.append(ref[pl.ds(at, 8), :])
        return jnp.concatenate(pieces, axis=1)

    groups = feats // 8
    z = jnp.concatenate([rows(group) for group in range(groups)], axis=0)
    solves = jnp.concatenate([rows(groups + g) for g in range(nprobe // 8)], axis=0)
    probes = jnp.concatenate([rows(groups + nprobe // 8 + g) for g in range(nprobe // 8)], axis=0)
    base = 8 * (groups + 2 * (nprobe // 8)) * tiles
    alpha = jnp.concatenate(
        [ref[pl.ds(base + first + tile, 1), :] for tile in range(wide // 128)], axis=1
    )
    return z, alpha, solves, probes


def fill_right(ref, chunk, sizes, right_q, right_c, zs):
    feats, nprobe, block = sizes
    z, alpha, solves, probes = chunk_of(ref, chunk, feats, nprobe, block)
    at = pl.ds(pl.multiple_of(chunk * wide, wide), wide)
    right_q[:, at] = distance_rows(z, True)
    right_c[:, at] = coef_rows(alpha, solves, probes, True)
    zs[:, at] = stack_rows(z)


def fill_left(ref, chunk, sizes, left_q, left_c):
    feats, nprobe, block = sizes
    z, alpha, solves, probes = chunk_of(ref, chunk, feats, nprobe, block)
    at = pl.ds(pl.multiple_of(chunk * wide, wide), wide)
    left_q[at, :] = distance_rows(z, False).T
    left_c[at, :] = coef_rows(alpha, solves, probes, False).T


def products(left_q, left_c, right_q, right_c, at_j, at_i):
    squared = jnp.dot(left_q[at_j, :], right_q[:, at_i], preferred_element_type=f32)
    coef = jnp.dot(left_c[at_j, :], right_c[:, at_i], preferred_element_type=f32)
    return squared, coef


def weigh(squared, coef):
    squared = jnp.maximum(squared, 1e-30)
    radius = squared * lax.rsqrt(squared)
    rest = jnp.maximum(1.0 - radius, 0.0)
    return rest * rest * rest * coef


def weights(left_q, left_c, right_q, right_c, at_j, at_i):
    return weigh(*products(left_q, left_c, right_q, right_c, at_j, at_i))


over_lanes = (((1,), (1,)), ((), ()))


def add_right(total, zs, at_j, at_i, high, low):
    total[:, at_i] += jnp.dot(zs[:, at_j], high, preferred_element_type=f32)
    total[:short, at_i] += jnp.dot(zs[:short, at_j], low, preferred_element_type=f32)


def add_left(total, zst, at_j, at_i, high, low):
    z = zst[at_i, :]
    both = jnp.concatenate([high, low], axis=1)
    total[at_j, :] += jnp.dot(both, jnp.concatenate([z, z], axis=0), preferred_element_type=f32)


def fill_stack_t(zst, zs, chunk):
    at = pl.ds(pl.multiple_of(chunk * wide, wide), wide)
    pad = jnp.zeros((128 - stack, wide), bf16)
    zst[at, :] = jnp.concatenate([zs[:, at], pad], axis=0).T


def finish_left(z, total, feats):
    return finish(z, total[...].T, feats)


def finish(z, total, feats):
    return z * total[feats : feats + 1, :] - (total[:feats, :] + total[short : short + feats, :])


def at_chunk(index, size):
    return pl.ds(pl.multiple_of(index * size, size), size)


def pipeline(first, steps, begin, use, even, odd):
    def store(slot, parts):
        high, low = split2(weigh(*parts))
        slot[0][...] = high
        slot[1][...] = low

    def two(pair, carry):
        step = first + 2 * pair
        parts = begin(step + 1)
        use(step, even)
        store(odd, parts)
        parts = begin(step + 2)
        use(step + 1, odd)
        store(even, parts)
        return carry

    def four(quad, carry):
        two(2 * quad, carry)
        return two(2 * quad + 1, carry)

    pairs = (steps - 1) // 2
    last = first + steps - 1
    store(even, begin(first))
    lax.fori_loop(0, pairs // 2, four, 0)
    lax.fori_loop(pairs // 2 * 2, pairs, two, 0)

    @pl.when(steps == 2 * pairs + 2)
    def _():
        parts = begin(last)
        use(last - 1, even)
        store(odd, parts)
        use(last, odd)

    @pl.when(steps == 2 * pairs + 1)
    def _():
        use(last, even)


def steps_of(count, size):
    return (count + size - 1) // size


def live_flag(mask, offset):
    band = (mask.shape[1] - 1) // 2
    return jnp.where(mask[0, band + owner_side[offset] * offset] > 0, 1, 0)


def own_range(counts, mask):
    steps_i, steps_j = steps_of(counts[0], step_i), steps_of(counts[0], step_j)
    core = lax.axis_index("col")
    loads = [sum(live_flag(mask, offsets[which]) for offsets in rounds) for which in range(2)]
    steps = steps_i * steps_j
    half = steps // 2
    mine = jnp.where(core == 0, loads[0], loads[1])
    theirs = jnp.where(core == 0, loads[1], loads[0])
    first = jnp.where((mine == theirs) & (core == 1), half, 0)
    end = jnp.where((mine == theirs) & (core == 0), half, jnp.where(mine > theirs, 0, steps))
    return first, jnp.maximum(first, end), steps_j


def own_steps(first, end, steps_j, left_q, left_c, right_q, right_c, zs, total, slots):
    def places(step):
        i = step // steps_j
        return at_chunk(step - i * steps_j, step_j), at_chunk(i, step_i)

    def begin(step):
        return products(left_q, left_c, right_q, right_c, *places(step))

    def use(step, slot):
        at_j, at_i = places(step)
        add_right(total, zs, at_j, at_i, slot[0][...], slot[1][...])

    @pl.when(end > first)
    def _():
        pipeline(first, end - first, begin, use, slots[:2], slots[2:])


def own_kernel(sizes, counts, mask, packed, left_q, left_c, zs, zf, right_q, right_c, total, *slots):
    feats, nprobe, block = sizes
    first, end, steps_j = own_range(counts, mask)
    for chunk in range(block // wide):
        zf[:, chunk * wide : chunk * wide + wide] = chunk_of(packed, chunk, feats, nprobe, block)[0]

    def prepare(chunk, carry):
        fill_left(packed, chunk, sizes, left_q, left_c)
        fill_right(packed, chunk, sizes, right_q, right_c, zs)
        return carry

    lax.fori_loop(0, steps_j * (step_j // wide), prepare, 0)
    total[...] = jnp.zeros_like(total)
    end = jnp.minimum(end, first + early)
    own_steps(first, end, steps_j, left_q, left_c, right_q, right_c, zs, total, slots)


def rest_kernel(sizes, counts, mask, left_q, left_c, zs, zf, right_q, right_c, total_in, grad, total, *slots):
    feats = sizes[0]
    first, end, steps_j = own_range(counts, mask)
    total[...] = total_in[...]
    own_steps(first + early, end, steps_j, left_q, left_c, right_q, right_c, zs, total, slots)
    grad[...] = finish(zf[...], total[...], feats)


def pair_kernel(
    sizes, offsets, counts, mask, packed, left_q, left_c, zs, zf, grad_in, grad, back, right_q, right_c, zsp, zfp, total, totalp, zst, *slots
):
    feats, nprobe, block = sizes
    base = packed.shape[0] - 8
    other = jnp.max(packed[base : base + 8, :]).astype(jnp.int32)
    live = jnp.where(lax.axis_index("col") == 0, live_flag(mask, offsets[0]), live_flag(mask, offsets[1]))
    steps_i = live * steps_of(other, step_i)
    steps_j = steps_of(counts[0], step_j)

    @pl.when(steps_i == 0)
    def _():
        grad[...] = grad_in[...]
        back[...] = jnp.zeros_like(back)

    @pl.when(steps_i > 0)
    def _():
        total[...] = jnp.zeros_like(total)
        totalp[...] = jnp.zeros_like(totalp)
        for chunk in range(block // wide):
            zfp[:, chunk * wide : chunk * wide + wide] = chunk_of(packed, chunk, feats, nprobe, block)[0]

        def prepare(chunk, carry):
            fill_right(packed, chunk, sizes, right_q, right_c, zsp)
            fill_stack_t(zst, zsp, chunk)
            return carry

        lax.fori_loop(0, steps_i * (step_i // wide), prepare, 0)

        def places(step):
            i = step // steps_j
            return at_chunk(step - i * steps_j, step_j), at_chunk(i, step_i)

        def begin(step):
            return products(left_q, left_c, right_q, right_c, *places(step))

        def use(step, slot):
            at_j, at_i = places(step)
            high, low = slot[0][...], slot[1][...]
            add_right(totalp, zs, at_j, at_i, high, low)
            add_left(total, zst, at_j, at_i, high, low)

        pipeline(0, steps_i * steps_j, begin, use, slots[:2], slots[2:])
        grad[...] = grad_in[...] + finish_left(zf[...], total, feats)
        back[...] = finish(zfp[...], totalp[...], feats)


def shape(*dims, dtype=f32):
    return jax.ShapeDtypeStruct(dims, dtype)


params = pltpu.CompilerParams(vmem_limit_bytes=32 << 20)
estimate = pl.CostEstimate(flops=8 << 30, bytes_accessed=4 << 20, transcendentals=2 << 20)


slot_scratch = [pltpu.VMEM((step_j, step_i), bf16)] * 4


def call_own(counts, mask, packed, sizes):
    feats, nprobe, block = sizes
    return pl.pallas_call(
        functools.partial(own_kernel, sizes),
        out_shape=(
            shape(block, depth_q, dtype=bf16),
            shape(block, depth_c, dtype=bf16),
            shape(stack, block, dtype=bf16),
            shape(feats, block),
            shape(depth_q, block, dtype=bf16),
            shape(depth_c, block, dtype=bf16),
            shape(stack, block),
        ),
        in_specs=smem(2) + vmem(1),
        out_specs=tuple(vmem(7)),
        scratch_shapes=slot_scratch,
        compiler_params=params,
        cost_estimate=estimate,
        name="own_tile",
    )(counts, mask, packed)


def call_rest(counts, mask, own, sizes):
    feats, nprobe, block = sizes
    return pl.pallas_call(
        functools.partial(rest_kernel, sizes),
        out_shape=shape(feats, block),
        in_specs=smem(2) + vmem(7),
        out_specs=vmem(1)[0],
        scratch_shapes=[pltpu.VMEM((stack, block), f32)] + slot_scratch,
        compiler_params=params,
        cost_estimate=estimate,
        name="own_rest",
    )(counts, mask, *own)


def call_pair(counts, mask, payload, own, grad, sizes, offsets):
    feats, nprobe, block = sizes
    return pl.pallas_call(
        functools.partial(pair_kernel, sizes, offsets),
        out_shape=(shape(feats, block), shape(feats, block)),
        in_specs=smem(2) + vmem(6),
        out_specs=tuple(vmem(2)),
        scratch_shapes=[
            pltpu.VMEM((depth_q, block), bf16),
            pltpu.VMEM((depth_c, block), bf16),
            pltpu.VMEM((stack, block), bf16),
            pltpu.VMEM((feats, block), f32),
            pltpu.VMEM((block, 128), f32),
            pltpu.VMEM((stack, block), f32),
            pltpu.VMEM((block, 128), bf16),
        ]
        + slot_scratch,
        compiler_params=params,
        cost_estimate=estimate,
        name="pair_tile",
    )(counts, mask, payload, *own, grad)


def pair_list(rows, cores, offsets, back):
    pairs = []
    for row in range(rows):
        for core in range(cores):
            offset = offsets[core]
            source = row + owner_side[offset] * offset
            if 0 <= source < rows:
                there, here = source * cores + core, row * cores + core
                pairs.append((here, there) if back else (there, here))
    return pairs


def local(embed, alpha_solve, probes, probe_solves, counts, tile_mask):
    feats, block = embed.shape[1:]
    sizes = (feats, probes.shape[1], block)
    rows, cores = lax.axis_size("row"), lax.axis_size("col")
    packed = call_pack(counts, embed, alpha_solve, probes, probe_solves)
    arrived = [lax.ppermute(packed, ("row", "col"), pair_list(rows, cores, rounds[0], False))]
    own = call_own(counts, tile_mask, packed, sizes)
    packed, own = lax.optimization_barrier((packed, own))
    arrived.append(lax.ppermute(packed, ("row", "col"), pair_list(rows, cores, rounds[1], False)))
    grad = call_rest(counts, tile_mask, own, sizes)
    own = own[:4]
    returned = []
    for offsets, payload in zip(rounds, arrived):
        grad, back = call_pair(counts, tile_mask, payload, own, grad, sizes, offsets)
        returned.append(lax.ppermute(back, ("row", "col"), pair_list(rows, cores, offsets, True)))
    total = grad + returned[0] + returned[1]
    total = total + lax.ppermute(total, "col", [(0, 1), (1, 0)])
    return total[None]


def solution(mesh):
    in_specs = (
        P(("grp", "row"), None, None),
        P(("grp", "row"), None),
        P(("grp", "row"), None, None),
        P(("grp", "row"), None, None),
        P(("grp", "row")),
        P(("grp", "row"), None),
    )
    out_specs = P(("grp", "row"), None, None)
    return jax.shard_map(local, mesh=mesh, in_specs=in_specs, out_specs=out_specs, check_vma=False)
```

```python
import functools

import jax
import jax.numpy as jnp
from jax import lax
from jax.experimental import pallas as pl
from jax.experimental.pallas import tpu as pltpu
from jax.sharding import PartitionSpec as P

lengthscale = 7.5
f32 = jnp.float32
bf16 = jnp.bfloat16

owner_side = {1: 1, 4: 1, 2: -1, 3: -1}
rounds = ((1, 2), (3, 4))

wide = 256
step_i = 256
step_j = 512
early = 6
depth_q = 256
depth_c = 128
stack = 80
short = 48


def vmem(count):
    return [pl.BlockSpec(memory_space=pltpu.VMEM)] * count


def smem(count):
    return [pl.BlockSpec(memory_space=pltpu.SMEM)] * count


def split3(value):
    high = value.astype(bf16)
    rest = value - high.astype(f32)
    mid = rest.astype(bf16)
    low = (rest - mid.astype(f32)).astype(bf16)
    return high, mid, low


def split2(value):
    high = value.astype(bf16)
    return high, (value - high.astype(f32)).astype(bf16)


def extra_rows(norms, norms_first):
    high, mid, low = (part.astype(f32) for part in split3(norms))
    width = norms.shape[1]
    index = lax.broadcasted_iota(jnp.int32, (16, width), 0)
    base = 0 if norms_first else 3
    one = 3 - base
    out = jnp.where((index >= one) & (index < one + 3), 1.0, 0.0)
    for place, part in enumerate((high, mid, low)):
        out = jnp.where(index == base + place, part, out)
    return out.astype(bf16)


def distance_rows(z, right):
    high, mid, low = split3(z)
    norms = jnp.sum(z * z, axis=0, keepdims=True)
    if right:
        high, mid, low = (part * jnp.asarray(-2.0, bf16) for part in (high, mid, low))
        parts = [high, mid, high, low, high, mid]
    else:
        parts = [high, high, mid, high, low, mid]
    pad = jnp.zeros((depth_q - 6 * z.shape[0] - 16, z.shape[1]), bf16)
    return jnp.concatenate(parts + [extra_rows(norms, not right), pad], axis=0)


def coef_rows(alpha, solves, probes, right):
    nprobe = probes.shape[0]
    width = probes.shape[1]
    pad = jnp.zeros((32 - 2 * nprobe - 8, width), f32)
    index = lax.broadcasted_iota(jnp.int32, (8, width), 0)
    if right:
        gain = -20.0 / lengthscale
        scale = -gain / (2.0 * nprobe)
        top = [scale * probes, scale * solves]
        alpha = gain * alpha
    else:
        top = [solves, probes]
    last = jnp.where(index == 0, alpha, 0.0)
    value = jnp.concatenate(top + [last, pad], axis=0)
    high, low = split2(value)
    parts = [high, low, high] if right else [high, high, low]
    fill = jnp.zeros((depth_c - 96, width), bf16)
    return jnp.concatenate(parts + [fill], axis=0)


def stack_rows(z):
    high, low = split2(z)
    index = lax.broadcasted_iota(jnp.int32, (16, z.shape[1]), 0)
    ones = jnp.where(index == 0, 1.0, 0.0).astype(bf16)
    return jnp.concatenate([high, ones, low], axis=0)


def pack_kernel(count_hbm, embed_hbm, alpha_hbm, probes_hbm, solves_hbm, out_ref, *scratch):
    count_ref, embed_ref, alpha_ref, probes_ref, solves_ref, done = scratch
    sources = (count_hbm, embed_hbm, alpha_hbm, probes_hbm, solves_hbm)
    copies = [
        pltpu.make_async_copy(source, target, done.at[place])
        for place, (source, target) in enumerate(zip(sources, scratch[:5]))
    ]
    for copy in copies:
        copy.start()
    for copy in copies:
        copy.wait()
    tiles = embed_ref.shape[2] // 128
    count = count_ref[0]
    place = 0
    for ref, scale in ((embed_ref, 1.0 / lengthscale), (solves_ref, None), (probes_ref, None)):
        for group in range(ref.shape[1] // 8):
            for tile in range(tiles):
                value = ref[0, 8 * group : 8 * group + 8, 128 * tile : 128 * tile + 128]
                if scale is None:
                    index = lax.broadcasted_iota(jnp.int32, (8, 128), 1) + 128 * tile
                    value = jnp.where(index < count, value, 0.0)
                else:
                    value = value * scale
                out_ref[place : place + 8, :] = value
                place += 8
    for tile in range(tiles):
        value = alpha_ref[:, 128 * tile : 128 * tile + 128]
        index = lax.broadcasted_iota(jnp.int32, (1, 128), 1) + 128 * tile
        out_ref[place : place + 1, :] = jnp.where(index < count, value, 0.0)
        place += 1
    out_ref[place : place + 8, :] = jnp.full((8, 128), 1.0, f32) * count.astype(f32)


def call_pack(counts, embed, alpha_solve, probes, probe_solves):
    feats, block = embed.shape[1:]
    values = (embed, alpha_solve, probes, probe_solves)
    return pl.pallas_call(
        pack_kernel,
        out_shape=shape(packed_rows(feats, probes.shape[1], block), 128),
        in_specs=[pl.BlockSpec(memory_space=pltpu.HBM)] * 5,
        out_specs=pl.BlockSpec(memory_space=pltpu.VMEM),
        scratch_shapes=[pltpu.SMEM(counts.shape, jnp.int32)]
        + [pltpu.VMEM(value.shape, f32) for value in values]
        + [pltpu.SemaphoreType.DMA((5,))],
        compiler_params=pltpu.CompilerParams(vmem_limit_bytes=62 << 20),
        name="pack",
    )(counts, *values)


def packed_rows(feats, nprobe, block):
    return (feats + 2 * nprobe) * block // 128 + block // 128 + 8


def chunk_of(ref, chunk, feats, nprobe, block):
    tiles = block // 128
    first = chunk * (wide // 128)

    def rows(start):
        pieces = []
        for tile in range(wide // 128):
            at = pl.multiple_of(8 * (start * tiles + first + tile), 8)
            pieces.append(ref[pl.ds(at, 8), :])
        return jnp.concatenate(pieces, axis=1)

    groups = feats // 8
    z = jnp.concatenate([rows(group) for group in range(groups)], axis=0)
    solves = jnp.concatenate([rows(groups + g) for g in range(nprobe // 8)], axis=0)
    probes = jnp.concatenate([rows(groups + nprobe // 8 + g) for g in range(nprobe // 8)], axis=0)
    base = 8 * (groups + 2 * (nprobe // 8)) * tiles
    alpha = jnp.concatenate(
        [ref[pl.ds(base + first + tile, 1), :] for tile in range(wide // 128)], axis=1
    )
    return z, alpha, solves, probes


def fill_right(ref, chunk, sizes, right_q, right_c, zs):
    feats, nprobe, block = sizes
    z, alpha, solves, probes = chunk_of(ref, chunk, feats, nprobe, block)
    at = pl.ds(pl.multiple_of(chunk * wide, wide), wide)
    right_q[:, at] = distance_rows(z, True)
    right_c[:, at] = coef_rows(alpha, solves, probes, True)
    zs[:, at] = stack_rows(z)


def fill_left(ref, chunk, sizes, left_q, left_c):
    feats, nprobe, block = sizes
    z, alpha, solves, probes = chunk_of(ref, chunk, feats, nprobe, block)
    at = pl.ds(pl.multiple_of(chunk * wide, wide), wide)
    left_q[at, :] = distance_rows(z, False).T
    left_c[at, :] = coef_rows(alpha, solves, probes, False).T


def products(left_q, left_c, right_q, right_c, at_j, at_i):
    squared = jnp.dot(left_q[at_j, :], right_q[:, at_i], preferred_element_type=f32)
    coef = jnp.dot(left_c[at_j, :], right_c[:, at_i], preferred_element_type=f32)
    return squared, coef


def weigh(squared, coef):
    squared = jnp.maximum(squared, 1e-30)
    radius = squared * lax.rsqrt(squared)
    rest = jnp.maximum(1.0 - radius, 0.0)
    return rest * rest * rest * coef


def weights(left_q, left_c, right_q, right_c, at_j, at_i):
    return weigh(*products(left_q, left_c, right_q, right_c, at_j, at_i))


over_lanes = (((1,), (1,)), ((), ()))


def add_right(total, zs, at_j, at_i, high, low):
    total[:, at_i] += jnp.dot(zs[:, at_j], high, preferred_element_type=f32)
    total[:short, at_i] += jnp.dot(zs[:short, at_j], low, preferred_element_type=f32)


def add_left(total, zs, at_j, at_i, high, low):
    total[:, at_j] += lax.dot_general(zs[:, at_i], high, over_lanes, preferred_element_type=f32)
    total[:short, at_j] += lax.dot_general(
        zs[:short, at_i], low, over_lanes, preferred_element_type=f32
    )


def fill_stack_t(zst, zs, chunk):
    at = pl.ds(pl.multiple_of(chunk * wide, wide), wide)
    pad = jnp.zeros((128 - stack, wide), bf16)
    zst[at, :] = jnp.concatenate([zs[:, at], pad], axis=0).T


def finish_left(z, total, feats):
    return finish(z, total[...].T, feats)


def finish(z, total, feats):
    return z * total[feats : feats + 1, :] - (total[:feats, :] + total[short : short + feats, :])


def at_chunk(index, size):
    return pl.ds(pl.multiple_of(index * size, size), size)


def pipeline(first, steps, begin, use, even, odd):
    def store(slot, parts):
        high, low = split2(weigh(*parts))
        slot[0][...] = high
        slot[1][...] = low

    def two(pair, carry):
        step = first + 2 * pair
        parts = begin(step + 1)
        use(step, even)
        store(odd, parts)
        parts = begin(step + 2)
        use(step + 1, odd)
        store(even, parts)
        return carry

    def four(quad, carry):
        two(2 * quad, carry)
        return two(2 * quad + 1, carry)

    pairs = (steps - 1) // 2
    last = first + steps - 1
    store(even, begin(first))
    lax.fori_loop(0, pairs // 2, four, 0)
    lax.fori_loop(pairs // 2 * 2, pairs, two, 0)

    @pl.when(steps == 2 * pairs + 2)
    def _():
        parts = begin(last)
        use(last - 1, even)
        store(odd, parts)
        use(last, odd)

    @pl.when(steps == 2 * pairs + 1)
    def _():
        use(last, even)


def steps_of(count, size):
    return (count + size - 1) // size


def live_flag(mask, offset):
    band = (mask.shape[1] - 1) // 2
    return jnp.where(mask[0, band + owner_side[offset] * offset] > 0, 1, 0)


def own_range(counts, mask):
    steps_i, steps_j = steps_of(counts[0], step_i), steps_of(counts[0], step_j)
    core = lax.axis_index("col")
    loads = [sum(live_flag(mask, offsets[which]) for offsets in rounds) for which in range(2)]
    steps = steps_i * steps_j
    half = steps // 2
    mine = jnp.where(core == 0, loads[0], loads[1])
    theirs = jnp.where(core == 0, loads[1], loads[0])
    first = jnp.where((mine == theirs) & (core == 1), half, 0)
    end = jnp.where((mine == theirs) & (core == 0), half, jnp.where(mine > theirs, 0, steps))
    return first, jnp.maximum(first, end), steps_j


def own_steps(first, end, steps_j, left_q, left_c, right_q, right_c, zs, total, slots):
    def places(step):
        i = step // steps_j
        return at_chunk(step - i * steps_j, step_j), at_chunk(i, step_i)

    def begin(step):
        return products(left_q, left_c, right_q, right_c, *places(step))

    def use(step, slot):
        at_j, at_i = places(step)
        add_right(total, zs, at_j, at_i, slot[0][...], slot[1][...])

    @pl.when(end > first)
    def _():
        pipeline(first, end - first, begin, use, slots[:2], slots[2:])


def own_kernel(sizes, counts, mask, packed, left_q, left_c, zs, zf, right_q, right_c, total, *slots):
    feats, nprobe, block = sizes
    first, end, steps_j = own_range(counts, mask)
    for chunk in range(block // wide):
        zf[:, chunk * wide : chunk * wide + wide] = chunk_of(packed, chunk, feats, nprobe, block)[0]

    def prepare(chunk, carry):
        fill_left(packed, chunk, sizes, left_q, left_c)
        fill_right(packed, chunk, sizes, right_q, right_c, zs)
        return carry

    lax.fori_loop(0, steps_j * (step_j // wide), prepare, 0)
    total[...] = jnp.zeros_like(total)
    end = jnp.minimum(end, first + early)
    own_steps(first, end, steps_j, left_q, left_c, right_q, right_c, zs, total, slots)


def rest_kernel(sizes, counts, mask, left_q, left_c, zs, zf, right_q, right_c, total_in, grad, total, *slots):
    feats = sizes[0]
    first, end, steps_j = own_range(counts, mask)
    total[...] = total_in[...]
    own_steps(first + early, end, steps_j, left_q, left_c, right_q, right_c, zs, total, slots)
    grad[...] = finish(zf[...], total[...], feats)


def pair_kernel(
    sizes, offsets, counts, mask, packed, left_q, left_c, zs, zf, grad_in, grad, back, right_q, right_c, zsp, zfp, total, totalp, zst, *slots
):
    feats, nprobe, block = sizes
    base = packed.shape[0] - 8
    other = jnp.max(packed[base : base + 8, :]).astype(jnp.int32)
    live = jnp.where(lax.axis_index("col") == 0, live_flag(mask, offsets[0]), live_flag(mask, offsets[1]))
    steps_i = live * steps_of(other, step_i)
    steps_j = steps_of(counts[0], step_j)

    @pl.when(steps_i == 0)
    def _():
        grad[...] = grad_in[...]
        back[...] = jnp.zeros_like(back)

    @pl.when(steps_i > 0)
    def _():
        total[...] = jnp.zeros_like(total)
        totalp[...] = jnp.zeros_like(totalp)
        for chunk in range(block // wide):
            zfp[:, chunk * wide : chunk * wide + wide] = chunk_of(packed, chunk, feats, nprobe, block)[0]

        def prepare(chunk, carry):
            fill_right(packed, chunk, sizes, right_q, right_c, zsp)
            return carry

        lax.fori_loop(0, steps_i * (step_i // wide), prepare, 0)

        def places(step):
            i = step // steps_j
            return at_chunk(step - i * steps_j, step_j), at_chunk(i, step_i)

        def begin(step):
            return products(left_q, left_c, right_q, right_c, *places(step))

        def use(step, slot):
            at_j, at_i = places(step)
            high, low = slot[0][...], slot[1][...]
            add_right(totalp, zs, at_j, at_i, high, low)
            add_left(total, zsp, at_j, at_i, high, low)

        pipeline(0, steps_i * steps_j, begin, use, slots[:2], slots[2:])
        grad[...] = grad_in[...] + finish(zf[...], total[...], feats)
        back[...] = finish(zfp[...], totalp[...], feats)


def shape(*dims, dtype=f32):
    return jax.ShapeDtypeStruct(dims, dtype)


params = pltpu.CompilerParams(vmem_limit_bytes=32 << 20)
estimate = pl.CostEstimate(flops=8 << 30, bytes_accessed=4 << 20, transcendentals=2 << 20)


slot_scratch = [pltpu.VMEM((step_j, step_i), bf16)] * 4


def call_own(counts, mask, packed, sizes):
    feats, nprobe, block = sizes
    return pl.pallas_call(
        functools.partial(own_kernel, sizes),
        out_shape=(
            shape(block, depth_q, dtype=bf16),
            shape(block, depth_c, dtype=bf16),
            shape(stack, block, dtype=bf16),
            shape(feats, block),
            shape(depth_q, block, dtype=bf16),
            shape(depth_c, block, dtype=bf16),
            shape(stack, block),
        ),
        in_specs=smem(2) + vmem(1),
        out_specs=tuple(vmem(7)),
        scratch_shapes=slot_scratch,
        compiler_params=params,
        cost_estimate=estimate,
        name="own_tile",
    )(counts, mask, packed)


def call_rest(counts, mask, own, sizes):
    feats, nprobe, block = sizes
    return pl.pallas_call(
        functools.partial(rest_kernel, sizes),
        out_shape=shape(feats, block),
        in_specs=smem(2) + vmem(7),
        out_specs=vmem(1)[0],
        scratch_shapes=[pltpu.VMEM((stack, block), f32)] + slot_scratch,
        compiler_params=params,
        cost_estimate=estimate,
        name="own_rest",
    )(counts, mask, *own)


def call_pair(counts, mask, payload, own, grad, sizes, offsets):
    feats, nprobe, block = sizes
    return pl.pallas_call(
        functools.partial(pair_kernel, sizes, offsets),
        out_shape=(shape(feats, block), shape(feats, block)),
        in_specs=smem(2) + vmem(6),
        out_specs=tuple(vmem(2)),
        scratch_shapes=[
            pltpu.VMEM((depth_q, block), bf16),
            pltpu.VMEM((depth_c, block), bf16),
            pltpu.VMEM((stack, block), bf16),
            pltpu.VMEM((feats, block), f32),
            pltpu.VMEM((stack, block), f32),
            pltpu.VMEM((stack, block), f32),
            pltpu.VMEM((block, 128), bf16),
        ]
        + slot_scratch,
        compiler_params=params,
        cost_estimate=estimate,
        name="pair_tile",
    )(counts, mask, payload, *own, grad)


def pair_list(rows, cores, offsets, back):
    pairs = []
    for row in range(rows):
        for core in range(cores):
            offset = offsets[core]
            source = row + owner_side[offset] * offset
            if 0 <= source < rows:
                there, here = source * cores + core, row * cores + core
                pairs.append((here, there) if back else (there, here))
    return pairs


def local(embed, alpha_solve, probes, probe_solves, counts, tile_mask):
    feats, block = embed.shape[1:]
    sizes = (feats, probes.shape[1], block)
    rows, cores = lax.axis_size("row"), lax.axis_size("col")
    packed = call_pack(counts, embed, alpha_solve, probes, probe_solves)
    arrived = [lax.ppermute(packed, ("row", "col"), pair_list(rows, cores, rounds[0], False))]
    own = call_own(counts, tile_mask, packed, sizes)
    packed, own = lax.optimization_barrier((packed, own))
    arrived.append(lax.ppermute(packed, ("row", "col"), pair_list(rows, cores, rounds[1], False)))
    grad = call_rest(counts, tile_mask, own, sizes)
    own = own[:4]
    returned = []
    for offsets, payload in zip(rounds, arrived):
        grad, back = call_pair(counts, tile_mask, payload, own, grad, sizes, offsets)
        returned.append(lax.ppermute(back, ("row", "col"), pair_list(rows, cores, offsets, True)))
    total = grad + returned[0] + returned[1]
    total = total + lax.ppermute(total, "col", [(0, 1), (1, 0)])
    return total[None]


def solution(mesh):
    in_specs = (
        P(("grp", "row"), None, None),
        P(("grp", "row"), None),
        P(("grp", "row"), None, None),
        P(("grp", "row"), None, None),
        P(("grp", "row")),
        P(("grp", "row"), None),
    )
    out_specs = P(("grp", "row"), None, None)
    return jax.shard_map(local, mesh=mesh, in_specs=in_specs, out_specs=out_specs, check_vma=False)
```

```python
import functools

import jax
import jax.numpy as jnp
from jax import lax
from jax.experimental import pallas as pl
from jax.experimental.pallas import tpu as pltpu
from jax.sharding import PartitionSpec as P

lengthscale = 7.5
f32 = jnp.float32
bf16 = jnp.bfloat16

owner_side = {1: 1, 4: 1, 2: -1, 3: -1}
rounds = ((1, 2), (3, 4))

wide = 256
step_i = 256
step_j = 512
early = 10
depth_q = 256
depth_c = 128
stack = 80
short = 48


def vmem(count):
    return [pl.BlockSpec(memory_space=pltpu.VMEM)] * count


def smem(count):
    return [pl.BlockSpec(memory_space=pltpu.SMEM)] * count


def split3(value):
    high = value.astype(bf16)
    rest = value - high.astype(f32)
    mid = rest.astype(bf16)
    low = (rest - mid.astype(f32)).astype(bf16)
    return high, mid, low


def split2(value):
    high = value.astype(bf16)
    return high, (value - high.astype(f32)).astype(bf16)


def extra_rows(norms, norms_first):
    high, mid, low = (part.astype(f32) for part in split3(norms))
    width = norms.shape[1]
    index = lax.broadcasted_iota(jnp.int32, (16, width), 0)
    base = 0 if norms_first else 3
    one = 3 - base
    out = jnp.where((index >= one) & (index < one + 3), 1.0, 0.0)
    for place, part in enumerate((high, mid, low)):
        out = jnp.where(index == base + place, part, out)
    return out.astype(bf16)


def distance_rows(z, right):
    high, mid, low = split3(z)
    norms = jnp.sum(z * z, axis=0, keepdims=True)
    if right:
        high, mid, low = (part * jnp.asarray(-2.0, bf16) for part in (high, mid, low))
        parts = [high, mid, high, low, high, mid]
    else:
        parts = [high, high, mid, high, low, mid]
    pad = jnp.zeros((depth_q - 6 * z.shape[0] - 16, z.shape[1]), bf16)
    return jnp.concatenate(parts + [extra_rows(norms, not right), pad], axis=0)


def coef_rows(alpha, solves, probes, right):
    nprobe = probes.shape[0]
    width = probes.shape[1]
    pad = jnp.zeros((32 - 2 * nprobe - 8, width), f32)
    index = lax.broadcasted_iota(jnp.int32, (8, width), 0)
    if right:
        gain = -20.0 / lengthscale
        scale = -gain / (2.0 * nprobe)
        top = [scale * probes, scale * solves]
        alpha = gain * alpha
    else:
        top = [solves, probes]
    last = jnp.where(index == 0, alpha, 0.0)
    value = jnp.concatenate(top + [last, pad], axis=0)
    high, low = split2(value)
    parts = [high, low, high] if right else [high, high, low]
    fill = jnp.zeros((depth_c - 96, width), bf16)
    return jnp.concatenate(parts + [fill], axis=0)


def stack_rows(z):
    high, low = split2(z)
    index = lax.broadcasted_iota(jnp.int32, (16, z.shape[1]), 0)
    ones = jnp.where(index == 0, 1.0, 0.0).astype(bf16)
    return jnp.concatenate([high, ones, low], axis=0)


def pack_kernel(count_hbm, embed_hbm, alpha_hbm, probes_hbm, solves_hbm, out_ref, *scratch):
    count_ref, embed_ref, alpha_ref, probes_ref, solves_ref, done = scratch
    sources = (count_hbm, embed_hbm, alpha_hbm, probes_hbm, solves_hbm)
    copies = [
        pltpu.make_async_copy(source, target, done.at[place])
        for place, (source, target) in enumerate(zip(sources, scratch[:5]))
    ]
    for copy in copies:
        copy.start()
    for copy in copies:
        copy.wait()
    tiles = embed_ref.shape[2] // 128
    count = count_ref[0]
    place = 0
    for ref, scale in ((embed_ref, 1.0 / lengthscale), (solves_ref, None), (probes_ref, None)):
        for group in range(ref.shape[1] // 8):
            for tile in range(tiles):
                value = ref[0, 8 * group : 8 * group + 8, 128 * tile : 128 * tile + 128]
                if scale is None:
                    index = lax.broadcasted_iota(jnp.int32, (8, 128), 1) + 128 * tile
                    value = jnp.where(index < count, value, 0.0)
                else:
                    value = value * scale
                out_ref[place : place + 8, :] = value
                place += 8
    for tile in range(tiles):
        value = alpha_ref[:, 128 * tile : 128 * tile + 128]
        index = lax.broadcasted_iota(jnp.int32, (1, 128), 1) + 128 * tile
        out_ref[place : place + 1, :] = jnp.where(index < count, value, 0.0)
        place += 1
    out_ref[place : place + 8, :] = jnp.full((8, 128), 1.0, f32) * count.astype(f32)


def call_pack(counts, embed, alpha_solve, probes, probe_solves):
    feats, block = embed.shape[1:]
    values = (embed, alpha_solve, probes, probe_solves)
    return pl.pallas_call(
        pack_kernel,
        out_shape=shape(packed_rows(feats, probes.shape[1], block), 128),
        in_specs=[pl.BlockSpec(memory_space=pltpu.HBM)] * 5,
        out_specs=pl.BlockSpec(memory_space=pltpu.VMEM),
        scratch_shapes=[pltpu.SMEM(counts.shape, jnp.int32)]
        + [pltpu.VMEM(value.shape, f32) for value in values]
        + [pltpu.SemaphoreType.DMA((5,))],
        compiler_params=pltpu.CompilerParams(vmem_limit_bytes=62 << 20),
        name="pack",
    )(counts, *values)


def packed_rows(feats, nprobe, block):
    return (feats + 2 * nprobe) * block // 128 + block // 128 + 8


def chunk_of(ref, chunk, feats, nprobe, block):
    tiles = block // 128
    first = chunk * (wide // 128)

    def rows(start):
        pieces = []
        for tile in range(wide // 128):
            at = pl.multiple_of(8 * (start * tiles + first + tile), 8)
            pieces.append(ref[pl.ds(at, 8), :])
        return jnp.concatenate(pieces, axis=1)

    groups = feats // 8
    z = jnp.concatenate([rows(group) for group in range(groups)], axis=0)
    solves = jnp.concatenate([rows(groups + g) for g in range(nprobe // 8)], axis=0)
    probes = jnp.concatenate([rows(groups + nprobe // 8 + g) for g in range(nprobe // 8)], axis=0)
    base = 8 * (groups + 2 * (nprobe // 8)) * tiles
    alpha = jnp.concatenate(
        [ref[pl.ds(base + first + tile, 1), :] for tile in range(wide // 128)], axis=1
    )
    return z, alpha, solves, probes


def fill_right(ref, chunk, sizes, right_q, right_c, zs):
    feats, nprobe, block = sizes
    z, alpha, solves, probes = chunk_of(ref, chunk, feats, nprobe, block)
    at = pl.ds(pl.multiple_of(chunk * wide, wide), wide)
    right_q[:, at] = distance_rows(z, True)
    right_c[:, at] = coef_rows(alpha, solves, probes, True)
    zs[:, at] = stack_rows(z)


def fill_left(ref, chunk, sizes, left_q, left_c):
    feats, nprobe, block = sizes
    z, alpha, solves, probes = chunk_of(ref, chunk, feats, nprobe, block)
    at = pl.ds(pl.multiple_of(chunk * wide, wide), wide)
    left_q[at, :] = distance_rows(z, False).T
    left_c[at, :] = coef_rows(alpha, solves, probes, False).T


def products(left_q, left_c, right_q, right_c, at_j, at_i):
    squared = jnp.dot(left_q[at_j, :], right_q[:, at_i], preferred_element_type=f32)
    coef = jnp.dot(left_c[at_j, :], right_c[:, at_i], preferred_element_type=f32)
    return squared, coef


def weigh(squared, coef):
    squared = jnp.clip(squared, 1e-30, 1.0)
    rest = 1.0 - squared * lax.rsqrt(squared)
    return rest * rest * rest * coef


def weights(left_q, left_c, right_q, right_c, at_j, at_i):
    return weigh(*products(left_q, left_c, right_q, right_c, at_j, at_i))


over_lanes = (((1,), (1,)), ((), ()))


def add_right(total, zs, at_j, at_i, high, low):
    total[:, at_i] += jnp.dot(zs[:, at_j], high, preferred_element_type=f32)
    total[:short, at_i] += jnp.dot(zs[:short, at_j], low, preferred_element_type=f32)


def add_left(total, zs, at_j, at_i, high, low):
    total[:, at_j] += lax.dot_general(zs[:, at_i], high, over_lanes, preferred_element_type=f32)
    total[:short, at_j] += lax.dot_general(
        zs[:short, at_i], low, over_lanes, preferred_element_type=f32
    )


def fill_stack_t(zst, zs, chunk):
    at = pl.ds(pl.multiple_of(chunk * wide, wide), wide)
    pad = jnp.zeros((128 - stack, wide), bf16)
    zst[at, :] = jnp.concatenate([zs[:, at], pad], axis=0).T


def finish_left(z, total, feats):
    return finish(z, total[...].T, feats)


def finish(z, total, feats):
    return z * total[feats : feats + 1, :] - (total[:feats, :] + total[short : short + feats, :])


def at_chunk(index, size):
    return pl.ds(pl.multiple_of(index * size, size), size)


def pipeline(first, steps, begin, use, even, odd):
    def store(slot, parts):
        high, low = split2(weigh(*parts))
        slot[0][...] = high
        slot[1][...] = low

    def two(pair, carry):
        step = first + 2 * pair
        parts = begin(step + 1)
        use(step, even)
        store(odd, parts)
        parts = begin(step + 2)
        use(step + 1, odd)
        store(even, parts)
        return carry

    def four(quad, carry):
        two(2 * quad, carry)
        return two(2 * quad + 1, carry)

    pairs = (steps - 1) // 2
    last = first + steps - 1
    store(even, begin(first))
    lax.fori_loop(0, pairs // 2, four, 0)
    lax.fori_loop(pairs // 2 * 2, pairs, two, 0)

    @pl.when(steps == 2 * pairs + 2)
    def _():
        parts = begin(last)
        use(last - 1, even)
        store(odd, parts)
        use(last, odd)

    @pl.when(steps == 2 * pairs + 1)
    def _():
        use(last, even)


def steps_of(count, size):
    return (count + size - 1) // size


def live_flag(mask, offset):
    band = (mask.shape[1] - 1) // 2
    return jnp.where(mask[0, band + owner_side[offset] * offset] > 0, 1, 0)


def own_range(counts, mask):
    steps_i, steps_j = steps_of(counts[0], step_i), steps_of(counts[0], step_j)
    core = lax.axis_index("col")
    loads = [sum(live_flag(mask, offsets[which]) for offsets in rounds) for which in range(2)]
    steps = steps_i * steps_j
    half = steps // 2
    mine = jnp.where(core == 0, loads[0], loads[1])
    theirs = jnp.where(core == 0, loads[1], loads[0])
    first = jnp.where((mine == theirs) & (core == 1), half, 0)
    end = jnp.where((mine == theirs) & (core == 0), half, jnp.where(mine > theirs, 0, steps))
    return first, jnp.maximum(first, end), steps_j


def own_steps(first, end, steps_j, left_q, left_c, right_q, right_c, zs, total, slots):
    def places(step):
        i = step // steps_j
        return at_chunk(step - i * steps_j, step_j), at_chunk(i, step_i)

    def begin(step):
        return products(left_q, left_c, right_q, right_c, *places(step))

    def use(step, slot):
        at_j, at_i = places(step)
        add_right(total, zs, at_j, at_i, slot[0][...], slot[1][...])

    @pl.when(end > first)
    def _():
        pipeline(first, end - first, begin, use, slots[:2], slots[2:])


def own_kernel(sizes, counts, mask, packed, left_q, left_c, zs, zf, right_q, right_c, total, *slots):
    feats, nprobe, block = sizes
    first, end, steps_j = own_range(counts, mask)
    for chunk in range(block // wide):
        zf[:, chunk * wide : chunk * wide + wide] = chunk_of(packed, chunk, feats, nprobe, block)[0]

    def prepare(chunk, carry):
        fill_left(packed, chunk, sizes, left_q, left_c)
        fill_right(packed, chunk, sizes, right_q, right_c, zs)
        return carry

    lax.fori_loop(0, steps_j * (step_j // wide), prepare, 0)
    total[...] = jnp.zeros_like(total)
    end = jnp.minimum(end, first + early)
    own_steps(first, end, steps_j, left_q, left_c, right_q, right_c, zs, total, slots)


def rest_kernel(sizes, counts, mask, left_q, left_c, zs, zf, right_q, right_c, total_in, grad, total, *slots):
    feats = sizes[0]
    first, end, steps_j = own_range(counts, mask)
    total[...] = total_in[...]
    own_steps(first + early, end, steps_j, left_q, left_c, right_q, right_c, zs, total, slots)
    grad[...] = finish(zf[...], total[...], feats)


def pair_kernel(
    sizes, offsets, counts, mask, packed, left_q, left_c, zs, zf, grad_in, grad, back, right_q, right_c, zsp, zfp, total, totalp, zst, *slots
):
    feats, nprobe, block = sizes
    base = packed.shape[0] - 8
    other = jnp.max(packed[base : base + 8, :]).astype(jnp.int32)
    live = jnp.where(lax.axis_index("col") == 0, live_flag(mask, offsets[0]), live_flag(mask, offsets[1]))
    steps_i = live * steps_of(other, step_i)
    steps_j = steps_of(counts[0], step_j)

    @pl.when(steps_i == 0)
    def _():
        grad[...] = grad_in[...]
        back[...] = jnp.zeros_like(back)

    @pl.when(steps_i > 0)
    def _():
        total[...] = jnp.zeros_like(total)
        totalp[...] = jnp.zeros_like(totalp)
        for chunk in range(block // wide):
            zfp[:, chunk * wide : chunk * wide + wide] = chunk_of(packed, chunk, feats, nprobe, block)[0]

        def prepare(chunk, carry):
            fill_right(packed, chunk, sizes, right_q, right_c, zsp)
            return carry

        lax.fori_loop(0, steps_i * (step_i // wide), prepare, 0)

        def places(step):
            i = step // steps_j
            return at_chunk(step - i * steps_j, step_j), at_chunk(i, step_i)

        def begin(step):
            return products(left_q, left_c, right_q, right_c, *places(step))

        def use(step, slot):
            at_j, at_i = places(step)
            high, low = slot[0][...], slot[1][...]
            add_right(totalp, zs, at_j, at_i, high, low)
            add_left(total, zsp, at_j, at_i, high, low)

        pipeline(0, steps_i * steps_j, begin, use, slots[:2], slots[2:])
        grad[...] = grad_in[...] + finish(zf[...], total[...], feats)
        back[...] = finish(zfp[...], totalp[...], feats)


def shape(*dims, dtype=f32):
    return jax.ShapeDtypeStruct(dims, dtype)


params = pltpu.CompilerParams(vmem_limit_bytes=32 << 20)
estimate = pl.CostEstimate(flops=8 << 30, bytes_accessed=4 << 20, transcendentals=2 << 20)


slot_scratch = [pltpu.VMEM((step_j, step_i), bf16)] * 4


def call_own(counts, mask, packed, sizes):
    feats, nprobe, block = sizes
    return pl.pallas_call(
        functools.partial(own_kernel, sizes),
        out_shape=(
            shape(block, depth_q, dtype=bf16),
            shape(block, depth_c, dtype=bf16),
            shape(stack, block, dtype=bf16),
            shape(feats, block),
            shape(depth_q, block, dtype=bf16),
            shape(depth_c, block, dtype=bf16),
            shape(stack, block),
        ),
        in_specs=smem(2) + vmem(1),
        out_specs=tuple(vmem(7)),
        scratch_shapes=slot_scratch,
        compiler_params=params,
        cost_estimate=estimate,
        name="own_tile",
    )(counts, mask, packed)


def call_rest(counts, mask, own, sizes):
    feats, nprobe, block = sizes
    return pl.pallas_call(
        functools.partial(rest_kernel, sizes),
        out_shape=shape(feats, block),
        in_specs=smem(2) + vmem(7),
        out_specs=vmem(1)[0],
        scratch_shapes=[pltpu.VMEM((stack, block), f32)] + slot_scratch,
        compiler_params=params,
        cost_estimate=estimate,
        name="own_rest",
    )(counts, mask, *own)


def call_pair(counts, mask, payload, own, grad, sizes, offsets):
    feats, nprobe, block = sizes
    return pl.pallas_call(
        functools.partial(pair_kernel, sizes, offsets),
        out_shape=(shape(feats, block), shape(feats, block)),
        in_specs=smem(2) + vmem(6),
        out_specs=tuple(vmem(2)),
        scratch_shapes=[
            pltpu.VMEM((depth_q, block), bf16),
            pltpu.VMEM((depth_c, block), bf16),
            pltpu.VMEM((stack, block), bf16),
            pltpu.VMEM((feats, block), f32),
            pltpu.VMEM((stack, block), f32),
            pltpu.VMEM((stack, block), f32),
            pltpu.VMEM((block, 128), bf16),
        ]
        + slot_scratch,
        compiler_params=params,
        cost_estimate=estimate,
        name="pair_tile",
    )(counts, mask, payload, *own, grad)


def pair_list(rows, cores, offsets, back):
    pairs = []
    for row in range(rows):
        for core in range(cores):
            offset = offsets[core]
            source = row + owner_side[offset] * offset
            if 0 <= source < rows:
                there, here = source * cores + core, row * cores + core
                pairs.append((here, there) if back else (there, here))
    return pairs


def local(embed, alpha_solve, probes, probe_solves, counts, tile_mask):
    feats, block = embed.shape[1:]
    sizes = (feats, probes.shape[1], block)
    rows, cores = lax.axis_size("row"), lax.axis_size("col")
    packed = call_pack(counts, embed, alpha_solve, probes, probe_solves)
    arrived = [lax.ppermute(packed, ("row", "col"), pair_list(rows, cores, rounds[0], False))]
    own = call_own(counts, tile_mask, packed, sizes)
    packed, own = lax.optimization_barrier((packed, own))
    arrived.append(lax.ppermute(packed, ("row", "col"), pair_list(rows, cores, rounds[1], False)))
    grad = call_rest(counts, tile_mask, own, sizes)
    own = own[:4]
    returned = []
    for offsets, payload in zip(rounds, arrived):
        grad, back = call_pair(counts, tile_mask, payload, own, grad, sizes, offsets)
        returned.append(lax.ppermute(back, ("row", "col"), pair_list(rows, cores, offsets, True)))
    total = grad + returned[0] + returned[1]
    total = total + lax.ppermute(total, "col", [(0, 1), (1, 0)])
    return total[None]


def solution(mesh):
    in_specs = (
        P(("grp", "row"), None, None),
        P(("grp", "row"), None),
        P(("grp", "row"), None, None),
        P(("grp", "row"), None, None),
        P(("grp", "row")),
        P(("grp", "row"), None),
    )
    out_specs = P(("grp", "row"), None, None)
    return jax.shard_map(local, mesh=mesh, in_specs=in_specs, out_specs=out_specs, check_vma=False)
```

```python
import functools

import jax
import jax.numpy as jnp
from jax import lax
from jax.experimental import pallas as pl
from jax.experimental.pallas import tpu as pltpu
from jax.sharding import PartitionSpec as P

lengthscale = 7.5
f32 = jnp.float32
bf16 = jnp.bfloat16

owner_side = {1: 1, 4: 1, 2: -1, 3: -1}
rounds = ((1, 2), (3, 4))

wide = 512
step_i = 256
step_j = 512
early = 10
depth_q = 256
depth_c = 128
stack = 80
short = 48


def vmem(count):
    return [pl.BlockSpec(memory_space=pltpu.VMEM)] * count


def smem(count):
    return [pl.BlockSpec(memory_space=pltpu.SMEM)] * count


def split3(value):
    high = value.astype(bf16)
    rest = value - high.astype(f32)
    mid = rest.astype(bf16)
    low = (rest - mid.astype(f32)).astype(bf16)
    return high, mid, low


def split2(value):
    high = value.astype(bf16)
    return high, (value - high.astype(f32)).astype(bf16)


def extra_rows(norms, norms_first):
    high, mid, low = (part.astype(f32) for part in split3(norms))
    width = norms.shape[1]
    index = lax.broadcasted_iota(jnp.int32, (16, width), 0)
    base = 0 if norms_first else 3
    one = 3 - base
    out = jnp.where((index >= one) & (index < one + 3), 1.0, 0.0)
    for place, part in enumerate((high, mid, low)):
        out = jnp.where(index == base + place, part, out)
    return out.astype(bf16)


def distance_rows(z, right):
    high, mid, low = split3(z)
    norms = jnp.sum(z * z, axis=0, keepdims=True)
    if right:
        high, mid, low = (part * jnp.asarray(-2.0, bf16) for part in (high, mid, low))
        parts = [high, mid, high, low, high, mid]
    else:
        parts = [high, high, mid, high, low, mid]
    pad = jnp.zeros((depth_q - 6 * z.shape[0] - 16, z.shape[1]), bf16)
    return jnp.concatenate(parts + [extra_rows(norms, not right), pad], axis=0)


def coef_rows(alpha, solves, probes, right):
    nprobe = probes.shape[0]
    width = probes.shape[1]
    pad = jnp.zeros((32 - 2 * nprobe - 8, width), f32)
    index = lax.broadcasted_iota(jnp.int32, (8, width), 0)
    if right:
        gain = -20.0 / lengthscale
        scale = -gain / (2.0 * nprobe)
        top = [scale * probes, scale * solves]
        alpha = gain * alpha
    else:
        top = [solves, probes]
    last = jnp.where(index == 0, alpha, 0.0)
    value = jnp.concatenate(top + [last, pad], axis=0)
    high, low = split2(value)
    parts = [high, low, high] if right else [high, high, low]
    fill = jnp.zeros((depth_c - 96, width), bf16)
    return jnp.concatenate(parts + [fill], axis=0)


def stack_rows(z):
    high, low = split2(z)
    index = lax.broadcasted_iota(jnp.int32, (16, z.shape[1]), 0)
    ones = jnp.where(index == 0, 1.0, 0.0).astype(bf16)
    return jnp.concatenate([high, ones, low], axis=0)


def pack_kernel(count_hbm, embed_hbm, alpha_hbm, probes_hbm, solves_hbm, out_ref, *scratch):
    count_ref, embed_ref, alpha_ref, probes_ref, solves_ref, done = scratch
    sources = (count_hbm, embed_hbm, alpha_hbm, probes_hbm, solves_hbm)
    copies = [
        pltpu.make_async_copy(source, target, done.at[place])
        for place, (source, target) in enumerate(zip(sources, scratch[:5]))
    ]
    for copy in copies:
        copy.start()
    for copy in copies:
        copy.wait()
    tiles = embed_ref.shape[2] // 128
    count = count_ref[0]
    place = 0
    for ref, scale in ((embed_ref, 1.0 / lengthscale), (solves_ref, None), (probes_ref, None)):
        for group in range(ref.shape[1] // 8):
            for tile in range(tiles):
                value = ref[0, 8 * group : 8 * group + 8, 128 * tile : 128 * tile + 128]
                if scale is None:
                    index = lax.broadcasted_iota(jnp.int32, (8, 128), 1) + 128 * tile
                    value = jnp.where(index < count, value, 0.0)
                else:
                    value = value * scale
                out_ref[place : place + 8, :] = value
                place += 8
    for tile in range(tiles):
        value = alpha_ref[:, 128 * tile : 128 * tile + 128]
        index = lax.broadcasted_iota(jnp.int32, (1, 128), 1) + 128 * tile
        out_ref[place : place + 1, :] = jnp.where(index < count, value, 0.0)
        place += 1
    out_ref[place : place + 8, :] = jnp.full((8, 128), 1.0, f32) * count.astype(f32)


def call_pack(counts, embed, alpha_solve, probes, probe_solves):
    feats, block = embed.shape[1:]
    values = (embed, alpha_solve, probes, probe_solves)
    return pl.pallas_call(
        pack_kernel,
        out_shape=shape(packed_rows(feats, probes.shape[1], block), 128),
        in_specs=[pl.BlockSpec(memory_space=pltpu.HBM)] * 5,
        out_specs=pl.BlockSpec(memory_space=pltpu.VMEM),
        scratch_shapes=[pltpu.SMEM(counts.shape, jnp.int32)]
        + [pltpu.VMEM(value.shape, f32) for value in values]
        + [pltpu.SemaphoreType.DMA((5,))],
        compiler_params=pltpu.CompilerParams(vmem_limit_bytes=62 << 20),
        name="pack",
    )(counts, *values)


def packed_rows(feats, nprobe, block):
    return (feats + 2 * nprobe) * block // 128 + block // 128 + 8


def chunk_of(ref, chunk, feats, nprobe, block):
    tiles = block // 128
    first = chunk * (wide // 128)

    def rows(start):
        pieces = []
        for tile in range(wide // 128):
            at = pl.multiple_of(8 * (start * tiles + first + tile), 8)
            pieces.append(ref[pl.ds(at, 8), :])
        return jnp.concatenate(pieces, axis=1)

    groups = feats // 8
    z = jnp.concatenate([rows(group) for group in range(groups)], axis=0)
    solves = jnp.concatenate([rows(groups + g) for g in range(nprobe // 8)], axis=0)
    probes = jnp.concatenate([rows(groups + nprobe // 8 + g) for g in range(nprobe // 8)], axis=0)
    base = 8 * (groups + 2 * (nprobe // 8)) * tiles
    alpha = jnp.concatenate(
        [ref[pl.ds(base + first + tile, 1), :] for tile in range(wide // 128)], axis=1
    )
    return z, alpha, solves, probes


def fill_right(ref, chunk, sizes, right_q, right_c, zs):
    feats, nprobe, block = sizes
    z, alpha, solves, probes = chunk_of(ref, chunk, feats, nprobe, block)
    at = pl.ds(pl.multiple_of(chunk * wide, wide), wide)
    right_q[:, at] = distance_rows(z, True)
    right_c[:, at] = coef_rows(alpha, solves, probes, True)
    zs[:, at] = stack_rows(z)


def fill_left(ref, chunk, sizes, left_q, left_c):
    feats, nprobe, block = sizes
    z, alpha, solves, probes = chunk_of(ref, chunk, feats, nprobe, block)
    at = pl.ds(pl.multiple_of(chunk * wide, wide), wide)
    left_q[at, :] = distance_rows(z, False).T
    left_c[at, :] = coef_rows(alpha, solves, probes, False).T


def products(left_q, left_c, right_q, right_c, at_j, at_i):
    squared = jnp.dot(left_q[at_j, :], right_q[:, at_i], preferred_element_type=f32)
    coef = jnp.dot(left_c[at_j, :], right_c[:, at_i], preferred_element_type=f32)
    return squared, coef


def weigh(squared, coef):
    squared = jnp.clip(squared, 1e-30, 1.0)
    rest = 1.0 - squared * lax.rsqrt(squared)
    return rest * rest * rest * coef


def weights(left_q, left_c, right_q, right_c, at_j, at_i):
    return weigh(*products(left_q, left_c, right_q, right_c, at_j, at_i))


over_lanes = (((1,), (1,)), ((), ()))


def add_right(total, zs, at_j, at_i, high, low):
    total[:, at_i] += jnp.dot(zs[:, at_j], high, preferred_element_type=f32)
    total[:short, at_i] += jnp.dot(zs[:short, at_j], low, preferred_element_type=f32)


def add_left(total, zs, at_j, at_i, high, low):
    total[:, at_j] += lax.dot_general(zs[:, at_i], high, over_lanes, preferred_element_type=f32)
    total[:short, at_j] += lax.dot_general(
        zs[:short, at_i], low, over_lanes, preferred_element_type=f32
    )


def fill_stack_t(zst, zs, chunk):
    at = pl.ds(pl.multiple_of(chunk * wide, wide), wide)
    pad = jnp.zeros((128 - stack, wide), bf16)
    zst[at, :] = jnp.concatenate([zs[:, at], pad], axis=0).T


def finish_left(z, total, feats):
    return finish(z, total[...].T, feats)


def finish(z, total, feats):
    return z * total[feats : feats + 1, :] - (total[:feats, :] + total[short : short + feats, :])


def at_chunk(index, size):
    return pl.ds(pl.multiple_of(index * size, size), size)


def pipeline(first, steps, begin, use, even, odd):
    def store(slot, parts):
        high, low = split2(weigh(*parts))
        slot[0][...] = high
        slot[1][...] = low

    def two(pair, carry):
        step = first + 2 * pair
        parts = begin(step + 1)
        use(step, even)
        store(odd, parts)
        parts = begin(step + 2)
        use(step + 1, odd)
        store(even, parts)
        return carry

    def four(quad, carry):
        two(2 * quad, carry)
        return two(2 * quad + 1, carry)

    pairs = (steps - 1) // 2
    last = first + steps - 1
    store(even, begin(first))
    lax.fori_loop(0, pairs // 2, four, 0)
    lax.fori_loop(pairs // 2 * 2, pairs, two, 0)

    @pl.when(steps == 2 * pairs + 2)
    def _():
        parts = begin(last)
        use(last - 1, even)
        store(odd, parts)
        use(last, odd)

    @pl.when(steps == 2 * pairs + 1)
    def _():
        use(last, even)


def steps_of(count, size):
    return (count + size - 1) // size


def live_flag(mask, offset):
    band = (mask.shape[1] - 1) // 2
    return jnp.where(mask[0, band + owner_side[offset] * offset] > 0, 1, 0)


def own_range(counts, mask):
    steps_i, steps_j = steps_of(counts[0], step_i), steps_of(counts[0], step_j)
    core = lax.axis_index("col")
    loads = [sum(live_flag(mask, offsets[which]) for offsets in rounds) for which in range(2)]
    steps = steps_i * steps_j
    half = steps // 2
    mine = jnp.where(core == 0, loads[0], loads[1])
    theirs = jnp.where(core == 0, loads[1], loads[0])
    first = jnp.where((mine == theirs) & (core == 1), half, 0)
    end = jnp.where((mine == theirs) & (core == 0), half, jnp.where(mine > theirs, 0, steps))
    return first, jnp.maximum(first, end), steps_j


def own_steps(first, end, steps_j, left_q, left_c, right_q, right_c, zs, total, slots):
    def places(step):
        i = step // steps_j
        return at_chunk(step - i * steps_j, step_j), at_chunk(i, step_i)

    def begin(step):
        return products(left_q, left_c, right_q, right_c, *places(step))

    def use(step, slot):
        at_j, at_i = places(step)
        add_right(total, zs, at_j, at_i, slot[0][...], slot[1][...])

    @pl.when(end > first)
    def _():
        pipeline(first, end - first, begin, use, slots[:2], slots[2:])


def own_kernel(sizes, counts, mask, packed, left_q, left_c, zs, zf, right_q, right_c, total, *slots):
    feats, nprobe, block = sizes
    first, end, steps_j = own_range(counts, mask)
    for chunk in range(block // wide):
        zf[:, chunk * wide : chunk * wide + wide] = chunk_of(packed, chunk, feats, nprobe, block)[0]

    def prepare(chunk, carry):
        fill_left(packed, chunk, sizes, left_q, left_c)
        fill_right(packed, chunk, sizes, right_q, right_c, zs)
        return carry

    lax.fori_loop(0, steps_of(steps_j * step_j, wide), prepare, 0)
    total[...] = jnp.zeros_like(total)
    end = jnp.minimum(end, first + early)
    own_steps(first, end, steps_j, left_q, left_c, right_q, right_c, zs, total, slots)


def rest_kernel(sizes, counts, mask, left_q, left_c, zs, zf, right_q, right_c, total_in, grad, total, *slots):
    feats = sizes[0]
    first, end, steps_j = own_range(counts, mask)
    total[...] = total_in[...]
    own_steps(first + early, end, steps_j, left_q, left_c, right_q, right_c, zs, total, slots)
    grad[...] = finish(zf[...], total[...], feats)


def pair_kernel(
    sizes, offsets, counts, mask, packed, left_q, left_c, zs, zf, grad_in, grad, back, right_q, right_c, zsp, zfp, total, totalp, zst, *slots
):
    feats, nprobe, block = sizes
    base = packed.shape[0] - 8
    other = jnp.max(packed[base : base + 8, :]).astype(jnp.int32)
    live = jnp.where(lax.axis_index("col") == 0, live_flag(mask, offsets[0]), live_flag(mask, offsets[1]))
    steps_i = live * steps_of(other, step_i)
    steps_j = steps_of(counts[0], step_j)

    @pl.when(steps_i == 0)
    def _():
        grad[...] = grad_in[...]
        back[...] = jnp.zeros_like(back)

    @pl.when(steps_i > 0)
    def _():
        total[...] = jnp.zeros_like(total)
        totalp[...] = jnp.zeros_like(totalp)
        for chunk in range(block // wide):
            zfp[:, chunk * wide : chunk * wide + wide] = chunk_of(packed, chunk, feats, nprobe, block)[0]

        def prepare(chunk, carry):
            fill_right(packed, chunk, sizes, right_q, right_c, zsp)
            return carry

        lax.fori_loop(0, steps_of(steps_i * step_i, wide), prepare, 0)

        def places(step):
            i = step // steps_j
            return at_chunk(step - i * steps_j, step_j), at_chunk(i, step_i)

        def begin(step):
            return products(left_q, left_c, right_q, right_c, *places(step))

        def use(step, slot):
            at_j, at_i = places(step)
            high, low = slot[0][...], slot[1][...]
            add_right(totalp, zs, at_j, at_i, high, low)
            add_left(total, zsp, at_j, at_i, high, low)

        pipeline(0, steps_i * steps_j, begin, use, slots[:2], slots[2:])
        grad[...] = grad_in[...] + finish(zf[...], total[...], feats)
        back[...] = finish(zfp[...], totalp[...], feats)


def shape(*dims, dtype=f32):
    return jax.ShapeDtypeStruct(dims, dtype)


params = pltpu.CompilerParams(vmem_limit_bytes=32 << 20)
estimate = pl.CostEstimate(flops=8 << 30, bytes_accessed=4 << 20, transcendentals=2 << 20)


slot_scratch = [pltpu.VMEM((step_j, step_i), bf16)] * 4


def call_own(counts, mask, packed, sizes):
    feats, nprobe, block = sizes
    return pl.pallas_call(
        functools.partial(own_kernel, sizes),
        out_shape=(
            shape(block, depth_q, dtype=bf16),
            shape(block, depth_c, dtype=bf16),
            shape(stack, block, dtype=bf16),
            shape(feats, block),
            shape(depth_q, block, dtype=bf16),
            shape(depth_c, block, dtype=bf16),
            shape(stack, block),
        ),
        in_specs=smem(2) + vmem(1),
        out_specs=tuple(vmem(7)),
        scratch_shapes=slot_scratch,
        compiler_params=params,
        cost_estimate=estimate,
        name="own_tile",
    )(counts, mask, packed)


def call_rest(counts, mask, own, sizes):
    feats, nprobe, block = sizes
    return pl.pallas_call(
        functools.partial(rest_kernel, sizes),
        out_shape=shape(feats, block),
        in_specs=smem(2) + vmem(7),
        out_specs=vmem(1)[0],
        scratch_shapes=[pltpu.VMEM((stack, block), f32)] + slot_scratch,
        compiler_params=params,
        cost_estimate=estimate,
        name="own_rest",
    )(counts, mask, *own)


def call_pair(counts, mask, payload, own, grad, sizes, offsets):
    feats, nprobe, block = sizes
    return pl.pallas_call(
        functools.partial(pair_kernel, sizes, offsets),
        out_shape=(shape(feats, block), shape(feats, block)),
        in_specs=smem(2) + vmem(6),
        out_specs=tuple(vmem(2)),
        scratch_shapes=[
            pltpu.VMEM((depth_q, block), bf16),
            pltpu.VMEM((depth_c, block), bf16),
            pltpu.VMEM((stack, block), bf16),
            pltpu.VMEM((feats, block), f32),
            pltpu.VMEM((stack, block), f32),
            pltpu.VMEM((stack, block), f32),
            pltpu.VMEM((block, 128), bf16),
        ]
        + slot_scratch,
        compiler_params=params,
        cost_estimate=estimate,
        name="pair_tile",
    )(counts, mask, payload, *own, grad)


def pair_list(rows, cores, offsets, back):
    pairs = []
    for row in range(rows):
        for core in range(cores):
            offset = offsets[core]
            source = row + owner_side[offset] * offset
            if 0 <= source < rows:
                there, here = source * cores + core, row * cores + core
                pairs.append((here, there) if back else (there, here))
    return pairs


def local(embed, alpha_solve, probes, probe_solves, counts, tile_mask):
    feats, block = embed.shape[1:]
    sizes = (feats, probes.shape[1], block)
    rows, cores = lax.axis_size("row"), lax.axis_size("col")
    packed = call_pack(counts, embed, alpha_solve, probes, probe_solves)
    arrived = [lax.ppermute(packed, ("row", "col"), pair_list(rows, cores, rounds[0], False))]
    own = call_own(counts, tile_mask, packed, sizes)
    packed, own = lax.optimization_barrier((packed, own))
    arrived.append(lax.ppermute(packed, ("row", "col"), pair_list(rows, cores, rounds[1], False)))
    grad = call_rest(counts, tile_mask, own, sizes)
    own = own[:4]
    returned = []
    for offsets, payload in zip(rounds, arrived):
        grad, back = call_pair(counts, tile_mask, payload, own, grad, sizes, offsets)
        returned.append(lax.ppermute(back, ("row", "col"), pair_list(rows, cores, offsets, True)))
    total = grad + returned[0] + returned[1]
    total = total + lax.ppermute(total, "col", [(0, 1), (1, 0)])
    return total[None]


def solution(mesh):
    in_specs = (
        P(("grp", "row"), None, None),
        P(("grp", "row"), None),
        P(("grp", "row"), None, None),
        P(("grp", "row"), None, None),
        P(("grp", "row")),
        P(("grp", "row"), None),
    )
    out_specs = P(("grp", "row"), None, None)
    return jax.shard_map(local, mesh=mesh, in_specs=in_specs, out_specs=out_specs, check_vma=False)
```

```python
import functools

import jax
import jax.numpy as jnp
from jax import lax
from jax.experimental import pallas as pl
from jax.experimental.pallas import tpu as pltpu
from jax.sharding import PartitionSpec as P

lengthscale = 7.5
f32 = jnp.float32
bf16 = jnp.bfloat16

owner_side = {1: 1, 4: 1, 2: -1, 3: -1}
rounds = ((1, 2), (3, 4))

wide = 512
step_i = 256
step_j = 512
early = 14
depth_q = 256
depth_c = 128
stack = 80
short = 48


def vmem(count):
    return [pl.BlockSpec(memory_space=pltpu.VMEM)] * count


def smem(count):
    return [pl.BlockSpec(memory_space=pltpu.SMEM)] * count


def split3(value):
    high = value.astype(bf16)
    rest = value - high.astype(f32)
    mid = rest.astype(bf16)
    low = (rest - mid.astype(f32)).astype(bf16)
    return high, mid, low


def split2(value):
    high = value.astype(bf16)
    return high, (value - high.astype(f32)).astype(bf16)


def extra_rows(norms, norms_first):
    high, mid, low = (part.astype(f32) for part in split3(norms))
    width = norms.shape[1]
    index = lax.broadcasted_iota(jnp.int32, (16, width), 0)
    base = 0 if norms_first else 3
    one = 3 - base
    out = jnp.where((index >= one) & (index < one + 3), 1.0, 0.0)
    for place, part in enumerate((high, mid, low)):
        out = jnp.where(index == base + place, part, out)
    return out.astype(bf16)


def distance_rows(z, right):
    high, mid, low = split3(z)
    norms = jnp.sum(z * z, axis=0, keepdims=True)
    if right:
        high, mid, low = (part * jnp.asarray(-2.0, bf16) for part in (high, mid, low))
        parts = [high, mid, high, low, high, mid]
    else:
        parts = [high, high, mid, high, low, mid]
    pad = jnp.zeros((depth_q - 6 * z.shape[0] - 16, z.shape[1]), bf16)
    return jnp.concatenate(parts + [extra_rows(norms, not right), pad], axis=0)


def coef_rows(alpha, solves, probes, right):
    nprobe = probes.shape[0]
    width = probes.shape[1]
    pad = jnp.zeros((32 - 2 * nprobe - 8, width), f32)
    index = lax.broadcasted_iota(jnp.int32, (8, width), 0)
    if right:
        gain = -20.0 / lengthscale
        scale = -gain / (2.0 * nprobe)
        top = [scale * probes, scale * solves]
        alpha = gain * alpha
    else:
        top = [solves, probes]
    last = jnp.where(index == 0, alpha, 0.0)
    value = jnp.concatenate(top + [last, pad], axis=0)
    high, low = split2(value)
    parts = [high, low, high] if right else [high, high, low]
    fill = jnp.zeros((depth_c - 96, width), bf16)
    return jnp.concatenate(parts + [fill], axis=0)


def stack_rows(z):
    high, low = split2(z)
    index = lax.broadcasted_iota(jnp.int32, (16, z.shape[1]), 0)
    ones = jnp.where(index == 0, 1.0, 0.0).astype(bf16)
    return jnp.concatenate([high, ones, low], axis=0)


def pack_kernel(count_hbm, embed_hbm, alpha_hbm, probes_hbm, solves_hbm, out_ref, *scratch):
    count_ref, embed_ref, alpha_ref, probes_ref, solves_ref, done = scratch
    sources = (count_hbm, embed_hbm, alpha_hbm, probes_hbm, solves_hbm)
    copies = [
        pltpu.make_async_copy(source, target, done.at[place])
        for place, (source, target) in enumerate(zip(sources, scratch[:5]))
    ]
    for copy in copies:
        copy.start()
    for copy in copies:
        copy.wait()
    tiles = embed_ref.shape[2] // 128
    count = count_ref[0]
    place = 0
    for ref, scale in ((embed_ref, 1.0 / lengthscale), (solves_ref, None), (probes_ref, None)):
        for group in range(ref.shape[1] // 8):
            for tile in range(tiles):
                value = ref[0, 8 * group : 8 * group + 8, 128 * tile : 128 * tile + 128]
                if scale is None:
                    index = lax.broadcasted_iota(jnp.int32, (8, 128), 1) + 128 * tile
                    value = jnp.where(index < count, value, 0.0)
                else:
                    value = value * scale
                out_ref[place : place + 8, :] = value
                place += 8
    for tile in range(tiles):
        value = alpha_ref[:, 128 * tile : 128 * tile + 128]
        index = lax.broadcasted_iota(jnp.int32, (1, 128), 1) + 128 * tile
        out_ref[place : place + 1, :] = jnp.where(index < count, value, 0.0)
        place += 1
    out_ref[place : place + 8, :] = jnp.full((8, 128), 1.0, f32) * count.astype(f32)


def call_pack(counts, embed, alpha_solve, probes, probe_solves):
    feats, block = embed.shape[1:]
    values = (embed, alpha_solve, probes, probe_solves)
    return pl.pallas_call(
        pack_kernel,
        out_shape=shape(packed_rows(feats, probes.shape[1], block), 128),
        in_specs=[pl.BlockSpec(memory_space=pltpu.HBM)] * 5,
        out_specs=pl.BlockSpec(memory_space=pltpu.VMEM),
        scratch_shapes=[pltpu.SMEM(counts.shape, jnp.int32)]
        + [pltpu.VMEM(value.shape, f32) for value in values]
        + [pltpu.SemaphoreType.DMA((5,))],
        compiler_params=pltpu.CompilerParams(vmem_limit_bytes=62 << 20),
        name="pack",
    )(counts, *values)


def packed_rows(feats, nprobe, block):
    return (feats + 2 * nprobe) * block // 128 + block // 128 + 8


def chunk_of(ref, chunk, feats, nprobe, block):
    tiles = block // 128
    first = chunk * (wide // 128)

    def rows(start):
        pieces = []
        for tile in range(wide // 128):
            at = pl.multiple_of(8 * (start * tiles + first + tile), 8)
            pieces.append(ref[pl.ds(at, 8), :])
        return jnp.concatenate(pieces, axis=1)

    groups = feats // 8
    z = jnp.concatenate([rows(group) for group in range(groups)], axis=0)
    solves = jnp.concatenate([rows(groups + g) for g in range(nprobe // 8)], axis=0)
    probes = jnp.concatenate([rows(groups + nprobe // 8 + g) for g in range(nprobe // 8)], axis=0)
    base = 8 * (groups + 2 * (nprobe // 8)) * tiles
    alpha = jnp.concatenate(
        [ref[pl.ds(base + first + tile, 1), :] for tile in range(wide // 128)], axis=1
    )
    return z, alpha, solves, probes


def fill_right(ref, chunk, sizes, right_q, right_c, zs):
    feats, nprobe, block = sizes
    z, alpha, solves, probes = chunk_of(ref, chunk, feats, nprobe, block)
    at = pl.ds(pl.multiple_of(chunk * wide, wide), wide)
    right_q[:, at] = distance_rows(z, True)
    right_c[:, at] = coef_rows(alpha, solves, probes, True)
    zs[:, at] = stack_rows(z)


def fill_left(ref, chunk, sizes, left_q, left_c):
    feats, nprobe, block = sizes
    z, alpha, solves, probes = chunk_of(ref, chunk, feats, nprobe, block)
    at = pl.ds(pl.multiple_of(chunk * wide, wide), wide)
    left_q[at, :] = distance_rows(z, False).T
    left_c[at, :] = coef_rows(alpha, solves, probes, False).T


def products(left_q, left_c, right_q, right_c, at_j, at_i):
    squared = jnp.dot(left_q[at_j, :], right_q[:, at_i], preferred_element_type=f32)
    coef = jnp.dot(left_c[at_j, :], right_c[:, at_i], preferred_element_type=f32)
    return squared, coef


def weigh(squared, coef):
    squared = jnp.clip(squared, 1e-30, 1.0)
    rest = 1.0 - squared * lax.rsqrt(squared)
    return rest * rest * rest * coef


def weights(left_q, left_c, right_q, right_c, at_j, at_i):
    return weigh(*products(left_q, left_c, right_q, right_c, at_j, at_i))


over_lanes = (((1,), (1,)), ((), ()))


def add_right(total, zs, at_j, at_i, high, low):
    total[:, at_i] += jnp.dot(zs[:, at_j], high, preferred_element_type=f32)
    total[:short, at_i] += jnp.dot(zs[:short, at_j], low, preferred_element_type=f32)


def add_left(total, zs, at_j, at_i, high, low):
    total[:, at_j] += lax.dot_general(zs[:, at_i], high, over_lanes, preferred_element_type=f32)
    total[:short, at_j] += lax.dot_general(
        zs[:short, at_i], low, over_lanes, preferred_element_type=f32
    )


def fill_stack_t(zst, zs, chunk):
    at = pl.ds(pl.multiple_of(chunk * wide, wide), wide)
    pad = jnp.zeros((128 - stack, wide), bf16)
    zst[at, :] = jnp.concatenate([zs[:, at], pad], axis=0).T


def finish_left(z, total, feats):
    return finish(z, total[...].T, feats)


def finish(z, total, feats):
    return z * total[feats : feats + 1, :] - (total[:feats, :] + total[short : short + feats, :])


def at_chunk(index, size):
    return pl.ds(pl.multiple_of(index * size, size), size)


def pipeline(first, steps, begin, use, even, odd):
    def store(slot, parts):
        high, low = split2(weigh(*parts))
        slot[0][...] = high
        slot[1][...] = low

    def two(pair, carry):
        step = first + 2 * pair
        parts = begin(step + 1)
        use(step, even)
        store(odd, parts)
        parts = begin(step + 2)
        use(step + 1, odd)
        store(even, parts)
        return carry

    def four(quad, carry):
        two(2 * quad, carry)
        return two(2 * quad + 1, carry)

    pairs = (steps - 1) // 2
    last = first + steps - 1
    store(even, begin(first))
    lax.fori_loop(0, pairs // 2, four, 0)
    lax.fori_loop(pairs // 2 * 2, pairs, two, 0)

    @pl.when(steps == 2 * pairs + 2)
    def _():
        parts = begin(last)
        use(last - 1, even)
        store(odd, parts)
        use(last, odd)

    @pl.when(steps == 2 * pairs + 1)
    def _():
        use(last, even)


def steps_of(count, size):
    return (count + size - 1) // size


def live_flag(mask, offset):
    band = (mask.shape[1] - 1) // 2
    return jnp.where(mask[0, band + owner_side[offset] * offset] > 0, 1, 0)


def own_range(counts, mask):
    steps_i, steps_j = steps_of(counts[0], step_i), steps_of(counts[0], step_j)
    core = lax.axis_index("col")
    loads = [sum(live_flag(mask, offsets[which]) for offsets in rounds) for which in range(2)]
    steps = steps_i * steps_j
    half = steps // 2
    mine = jnp.where(core == 0, loads[0], loads[1])
    theirs = jnp.where(core == 0, loads[1], loads[0])
    first = jnp.where((mine == theirs) & (core == 1), half, 0)
    end = jnp.where((mine == theirs) & (core == 0), half, jnp.where(mine > theirs, 0, steps))
    return first, jnp.maximum(first, end), steps_j


def own_steps(first, end, steps_j, left_q, left_c, right_q, right_c, zs, total, slots):
    def places(step):
        i = step // steps_j
        return at_chunk(step - i * steps_j, step_j), at_chunk(i, step_i)

    def begin(step):
        return products(left_q, left_c, right_q, right_c, *places(step))

    def use(step, slot):
        at_j, at_i = places(step)
        add_right(total, zs, at_j, at_i, slot[0][...], slot[1][...])

    @pl.when(end > first)
    def _():
        pipeline(first, end - first, begin, use, slots[:2], slots[2:])


def own_kernel(sizes, counts, mask, packed, left_q, left_c, zs, zf, right_q, right_c, total, *slots):
    feats, nprobe, block = sizes
    first, end, steps_j = own_range(counts, mask)
    for chunk in range(block // wide):
        zf[:, chunk * wide : chunk * wide + wide] = chunk_of(packed, chunk, feats, nprobe, block)[0]

    def prepare(chunk, carry):
        fill_left(packed, chunk, sizes, left_q, left_c)
        fill_right(packed, chunk, sizes, right_q, right_c, zs)
        return carry

    lax.fori_loop(0, steps_of(steps_j * step_j, wide), prepare, 0)
    total[...] = jnp.zeros_like(total)
    end = jnp.minimum(end, first + early)
    own_steps(first, end, steps_j, left_q, left_c, right_q, right_c, zs, total, slots)


def rest_kernel(sizes, counts, mask, left_q, left_c, zs, zf, right_q, right_c, total_in, grad, total, *slots):
    feats = sizes[0]
    first, end, steps_j = own_range(counts, mask)
    total[...] = total_in[...]
    own_steps(first + early, end, steps_j, left_q, left_c, right_q, right_c, zs, total, slots)
    grad[...] = finish(zf[...], total[...], feats)


def pair_kernel(
    sizes, offsets, counts, mask, packed, left_q, left_c, zs, zf, grad_in, grad, back, right_q, right_c, zsp, zfp, total, totalp, zst, *slots
):
    feats, nprobe, block = sizes
    base = packed.shape[0] - 8
    other = jnp.max(packed[base : base + 8, :]).astype(jnp.int32)
    live = jnp.where(lax.axis_index("col") == 0, live_flag(mask, offsets[0]), live_flag(mask, offsets[1]))
    steps_i = live * steps_of(other, step_i)
    steps_j = steps_of(counts[0], step_j)

    @pl.when(steps_i == 0)
    def _():
        grad[...] = grad_in[...]
        back[...] = jnp.zeros_like(back)

    @pl.when(steps_i > 0)
    def _():
        total[...] = jnp.zeros_like(total)
        totalp[...] = jnp.zeros_like(totalp)
        for chunk in range(block // wide):
            zfp[:, chunk * wide : chunk * wide + wide] = chunk_of(packed, chunk, feats, nprobe, block)[0]

        def prepare(chunk, carry):
            fill_right(packed, chunk, sizes, right_q, right_c, zsp)
            return carry

        lax.fori_loop(0, steps_of(steps_i * step_i, wide), prepare, 0)

        def places(step):
            i = step // steps_j
            return at_chunk(step - i * steps_j, step_j), at_chunk(i, step_i)

        def begin(step):
            return products(left_q, left_c, right_q, right_c, *places(step))

        def use(step, slot):
            at_j, at_i = places(step)
            high, low = slot[0][...], slot[1][...]
            add_right(totalp, zs, at_j, at_i, high, low)
            add_left(total, zsp, at_j, at_i, high, low)

        pipeline(0, steps_i * steps_j, begin, use, slots[:2], slots[2:])
        grad[...] = grad_in[...] + finish(zf[...], total[...], feats)
        back[...] = finish(zfp[...], totalp[...], feats)


def shape(*dims, dtype=f32):
    return jax.ShapeDtypeStruct(dims, dtype)


params = pltpu.CompilerParams(vmem_limit_bytes=32 << 20)
estimate = pl.CostEstimate(flops=8 << 30, bytes_accessed=4 << 20, transcendentals=2 << 20)


slot_scratch = [pltpu.VMEM((step_j, step_i), bf16)] * 4


def call_own(counts, mask, packed, sizes):
    feats, nprobe, block = sizes
    return pl.pallas_call(
        functools.partial(own_kernel, sizes),
        out_shape=(
            shape(block, depth_q, dtype=bf16),
            shape(block, depth_c, dtype=bf16),
            shape(stack, block, dtype=bf16),
            shape(feats, block),
            shape(depth_q, block, dtype=bf16),
            shape(depth_c, block, dtype=bf16),
            shape(stack, block),
        ),
        in_specs=smem(2) + vmem(1),
        out_specs=tuple(vmem(7)),
        scratch_shapes=slot_scratch,
        compiler_params=params,
        cost_estimate=estimate,
        name="own_tile",
    )(counts, mask, packed)


def call_rest(counts, mask, own, sizes):
    feats, nprobe, block = sizes
    return pl.pallas_call(
        functools.partial(rest_kernel, sizes),
        out_shape=shape(feats, block),
        in_specs=smem(2) + vmem(7),
        out_specs=vmem(1)[0],
        scratch_shapes=[pltpu.VMEM((stack, block), f32)] + slot_scratch,
        compiler_params=params,
        cost_estimate=estimate,
        name="own_rest",
    )(counts, mask, *own)


def call_pair(counts, mask, payload, own, grad, sizes, offsets):
    feats, nprobe, block = sizes
    return pl.pallas_call(
        functools.partial(pair_kernel, sizes, offsets),
        out_shape=(shape(feats, block), shape(feats, block)),
        in_specs=smem(2) + vmem(6),
        out_specs=tuple(vmem(2)),
        scratch_shapes=[
            pltpu.VMEM((depth_q, block), bf16),
            pltpu.VMEM((depth_c, block), bf16),
            pltpu.VMEM((stack, block), bf16),
            pltpu.VMEM((feats, block), f32),
            pltpu.VMEM((stack, block), f32),
            pltpu.VMEM((stack, block), f32),
            pltpu.VMEM((block, 128), bf16),
        ]
        + slot_scratch,
        compiler_params=params,
        cost_estimate=estimate,
        name="pair_tile",
    )(counts, mask, payload, *own, grad)


def pair_list(rows, cores, offsets, back):
    pairs = []
    for row in range(rows):
        for core in range(cores):
            offset = offsets[core]
            source = row + owner_side[offset] * offset
            if 0 <= source < rows:
                there, here = source * cores + core, row * cores + core
                pairs.append((here, there) if back else (there, here))
    return pairs


def local(embed, alpha_solve, probes, probe_solves, counts, tile_mask):
    feats, block = embed.shape[1:]
    sizes = (feats, probes.shape[1], block)
    rows, cores = lax.axis_size("row"), lax.axis_size("col")
    packed = call_pack(counts, embed, alpha_solve, probes, probe_solves)
    arrived = [lax.ppermute(packed, ("row", "col"), pair_list(rows, cores, rounds[0], False))]
    own = call_own(counts, tile_mask, packed, sizes)
    packed, own = lax.optimization_barrier((packed, own))
    arrived.append(lax.ppermute(packed, ("row", "col"), pair_list(rows, cores, rounds[1], False)))
    grad = call_rest(counts, tile_mask, own, sizes)
    own = own[:4]
    returned = []
    for offsets, payload in zip(rounds, arrived):
        grad, back = call_pair(counts, tile_mask, payload, own, grad, sizes, offsets)
        returned.append(lax.ppermute(back, ("row", "col"), pair_list(rows, cores, offsets, True)))
    total = grad + returned[0] + returned[1]
    total = total + lax.ppermute(total, "col", [(0, 1), (1, 0)])
    return total[None]


def solution(mesh):
    in_specs = (
        P(("grp", "row"), None, None),
        P(("grp", "row"), None),
        P(("grp", "row"), None, None),
        P(("grp", "row"), None, None),
        P(("grp", "row")),
        P(("grp", "row"), None),
    )
    out_specs = P(("grp", "row"), None, None)
    return jax.shard_map(local, mesh=mesh, in_specs=in_specs, out_specs=out_specs, check_vma=False)
```
